32 devices in a mesh: outer: 8 (over y, x, core), inner: 4 (over z).
Axes of the slice: x: 2, y: 2, z: 4, core: 2. Of those that a mesh axis runs over, the one named last changes fastest.
Arguments:
- photo_embedding_matrix: bfloat16 [4096, 1152], P(('outer', 'inner')), may hold values from -1 to 1
- sentence_embedding_matrix: bfloat16 [4096, 1152], P(('outer', 'inner')), may hold values from -1 to 1
- logit_stretch_factor: float32 [1], replicated, may hold values from 4 to 8
- logit_offset_term: float32 [1], replicated, may hold values from -4 to -2
Outputs:
- grad_image: float32 [4096, 1152], P(('outer', 'inner'))
- grad_text: float32 [4096, 1152], P(('outer', 'inner'))
The draws below stay inside these ranges and needn't reach their ends.
All inputs are finite; a program needn't handle non-finite values.
Results may differ from the reference program's by a relative error of at most 0.0027.
Values may be sent and summed in bfloat16 or wider, within the bound.
A program may use at most 64 MiB of HBM per device.

```python
import jax
import jax.numpy as jnp
from jax import lax

D = 1152
ROWS = 128
BATCH = 4096
N_OUTER = 8
N_INNER = 4


def shared_base(key):
    return jax.random.normal(jax.random.fold_in(key, 11), (BATCH, D), jnp.float32) * D ** (-0.5)


def draw_photo_embedding_matrix(key, part):
    base = shared_base(key)
    return jnp.clip(base, -1.0, 1.0).astype(jnp.bfloat16)


def draw_sentence_embedding_matrix(key, part):
    base = shared_base(key)
    key = jax.random.fold_in(key, 7)
    mixing = jax.random.uniform(jax.random.fold_in(key, 1), (BATCH, 1), jnp.float32, 0.0, 0.9)
    noise = jax.random.normal(jax.random.fold_in(key, 2), (BATCH, D), jnp.float32) * D ** (-0.5)
    return jnp.clip(mixing * base + jnp.sqrt(1.0 - mixing * mixing) * noise, -1.0, 1.0).astype(jnp.bfloat16)


def setup_inputs(seed: int = 0) -> dict:
    streams_of = jax.random.split(jax.random.key(seed), 5)
    return {
        "photo_embedding_matrix": draw_photo_embedding_matrix(jax.random.fold_in(streams_of[4], 71), 0),
        "sentence_embedding_matrix": draw_sentence_embedding_matrix(jax.random.fold_in(streams_of[4], 71), 0),
        "logit_stretch_factor": jnp.clip(jax.random.uniform(streams_of[2], (1,), jnp.float32, 4.0, 8.0), 4.0, 8.0),
        "logit_offset_term": jnp.clip(jax.random.uniform(streams_of[3], (1,), jnp.float32, -4.0, -2.0), -4.0, -2.0),
    }


def signed_multiplier(left_rows, right_rows, reciprocal_logit_temp, offset, positive):
    scores = reciprocal_logit_temp * lax.dot_general(left_rows, right_rows, (((1,), (1,)), ((), ())), preferred_element_type=jnp.float32) + offset
    signs = jnp.where(positive, 1.0, -1.0).astype(jnp.float32)
    return (-signs * jax.nn.sigmoid(-signs * scores) * reciprocal_logit_temp).astype(jnp.bfloat16)


def reference(photo_embedding_matrix, sentence_embedding_matrix, logit_stretch_factor, logit_offset_term):
    block_rows = ROWS * N_INNER
    reciprocal_logit_temp = logit_stretch_factor[0]
    offset = logit_offset_term[0]
    local_picture_rows = photo_embedding_matrix.reshape(N_OUTER, block_rows, D)
    next_images = jnp.roll(local_picture_rows, -1, axis=0)
    group_text = sentence_embedding_matrix.reshape(N_OUTER, block_rows, D)
    row_index = lax.broadcasted_iota(jnp.int32, (block_rows, block_rows), 0)
    column_position = lax.broadcasted_iota(jnp.int32, (block_rows, block_rows), 1)
    positive = row_index == column_position
    nothing = row_index < 0

    def per_group(items):
        mine, visiting_partner_blocks, texts = items
        own_coef = signed_multiplier(mine, texts, reciprocal_logit_temp, offset, positive)
        guest_coef = signed_multiplier(visiting_partner_blocks, texts, reciprocal_logit_temp, offset, nothing)
        own_grad = jnp.dot(own_coef, texts, preferred_element_type=jnp.float32)
        guest_grad = jnp.dot(guest_coef, texts, preferred_element_type=jnp.float32)
        sentence_slice_share = jnp.dot(own_coef.T, mine, preferred_element_type=jnp.float32)
        sentence_slice_share = sentence_slice_share + jnp.dot(guest_coef.T, visiting_partner_blocks, preferred_element_type=jnp.float32)
        return own_grad, guest_grad, sentence_slice_share

    own_grad, guest_grad, sentence_slice_share = lax.map(per_group, (local_picture_rows, next_images, group_text))
    grad_image = own_grad + jnp.roll(guest_grad, 1, axis=0)
    return grad_image.reshape(BATCH, D), sentence_slice_share.reshape(BATCH, D)
```

```python
import functools

import jax
import jax.numpy as jnp
from jax import lax
from jax.experimental import pallas as pl
from jax.experimental.pallas import tpu as pltpu
from jax.sharding import PartitionSpec as P

MESH = pl.DeviceIdType.MESH
TEXT, IMAGE = 0, 1


def kernel(
    n, m, image, text, scale, offset, grad_image, grad_text,
    own, group, guest, load_sem, line_send, line_recv, side_send, side_recv,
):
    outer, z = lax.axis_index("outer"), lax.axis_index("inner")
    above, below = lax.rem(outer + 1, m), lax.rem(outer + m - 1, m)
    rows = text.shape[0]
    source = (text, image)
    side = (above, below)

    loads = [pltpu.make_async_copy(source[k], own.at[k], load_sem.at[k]) for k in (TEXT, IMAGE)]
    for load in loads:
        load.start()

    barrier = pltpu.get_barrier_semaphore()

    def greet(o, i):
        pl.semaphore_signal(barrier, inc=1, device_id=(o, i), device_id_type=MESH)

    greet(above, z)
    greet(below, z)
    pl.when(z > 0)(lambda: greet(outer, z - 1))
    pl.when(z < n - 1)(lambda: greet(outer, z + 1))
    pl.semaphore_wait(barrier, 2 + (z > 0).astype(jnp.int32) + (z < n - 1).astype(jnp.int32))

    def along(k, src, slot, way):
        return pltpu.make_async_remote_copy(
            src_ref=src,
            dst_ref=group.at[k, slot],
            send_sem=line_send.at[k, slot, way],
            recv_sem=line_recv.at[k, slot],
            device_id=(outer, z + (1 if way else -1)),
            device_id_type=MESH,
        )

    def across(k, src, slot):
        return pltpu.make_async_remote_copy(
            src_ref=src,
            dst_ref=guest.at[k, slot],
            send_sem=side_send.at[k, slot],
            recv_sem=side_recv.at[k, slot],
            device_id=(side[k], z),
            device_id_type=MESH,
        )

    def has_next(way):
        return z < n - 1 if way else z > 0

    def add(k, block, first=False):
        out = (grad_image, grad_text)[k]
        product = lax.dot_general(
            own[1 - k], block[...], (((1,), (1,)), ((), ())), preferred_element_type=jnp.float32
        )
        logit = scale[0] * product + offset[0]
        if first:
            row = lax.broadcasted_iota(jnp.int32, (rows, rows), 0)
            column = lax.broadcasted_iota(jnp.int32, (rows, rows), 1)
            sign = jnp.where(row == column, 1.0, -1.0)
            coef = -sign * jax.nn.sigmoid(-sign * logit) * scale[0]
        else:
            coef = jax.nn.sigmoid(logit) * scale[0]
        term = jnp.dot(coef.astype(jnp.bfloat16), block[...], preferred_element_type=jnp.float32)
        out[...] = term if first else out[...] + term

    for k in (TEXT, IMAGE):
        for way in (1, 0):
            pl.when(has_next(way))(lambda: along(k, source[k], z, way).start())
        across(k, source[k], z).start()

    for load in loads:
        load.wait()
    for k in (TEXT, IMAGE):
        add(k, own.at[k], first=True)

    def visit(k, slot):
        across(k, guest.at[k, slot], slot).wait_recv()
        add(k, guest.at[k, slot])

    visit(TEXT, z)

    def step(s, _):
        def from_line(k):
            for way in (1, 0):
                slot = z - s if way else z + s

                @pl.when(slot >= 0 if way else slot < n)
                def _():
                    along(k, source[k], slot, way).wait_recv()
                    pl.when(has_next(way))(
                        lambda: along(k, group.at[k, slot], slot, way).start()
                    )
                    across(k, group.at[k, slot], slot).start()

            for way in (1, 0):
                slot = z - s if way else z + s
                pl.when(slot >= 0 if way else slot < n)(lambda: add(k, group.at[k, slot]))

        from_line(TEXT)
        pl.when(z - s + 1 >= 0)(lambda: visit(IMAGE, z - s + 1))
        pl.when((z + s - 1 < n) & (s > 1))(lambda: visit(IMAGE, z + s - 1))
        from_line(IMAGE)
        pl.when(z - s >= 0)(lambda: visit(TEXT, z - s))
        pl.when(z + s < n)(lambda: visit(TEXT, z + s))
        return 0

    lax.fori_loop(1, n, step, 0)
    if n > 1:
        pl.when(z - n + 1 >= 0)(lambda: visit(IMAGE, z - n + 1))
        pl.when(z + n - 1 < n)(lambda: visit(IMAGE, z + n - 1))

    def drain(slot, _):
        for k in (TEXT, IMAGE):
            across(k, source[k], slot).wait_send()
            pl.when((slot <= z) & (z < n - 1))(lambda: along(k, source[k], slot, 1).wait_send())
            pl.when((slot >= z) & (z > 0))(lambda: along(k, source[k], slot, 0).wait_send())
        return 0

    lax.fori_loop(0, n, drain, 0)


def solution(mesh):
    n, m = mesh.shape["inner"], mesh.shape["outer"]

    def per_device(image, text, scale, offset):
        rows, width = image.shape
        dma = pltpu.SemaphoreType.DMA
        return pl.pallas_call(
            functools.partial(kernel, n, m),
            out_shape=(jax.ShapeDtypeStruct((rows, width), jnp.float32),) * 2,
            in_specs=[pl.BlockSpec(memory_space=pl.ANY)] * 2
            + [pl.BlockSpec(memory_space=pltpu.SMEM)] * 2,
            out_specs=(pl.BlockSpec(memory_space=pltpu.VMEM),) * 2,
            scratch_shapes=[
                pltpu.VMEM((2, rows, width), jnp.bfloat16),
                pltpu.VMEM((2, n, rows, width), jnp.bfloat16),
                pltpu.VMEM((2, n, rows, width), jnp.bfloat16),
                dma((2,)),
                dma((2, n, 2)),
                dma((2, n)),
                dma((2, n)),
                dma((2, n)),
            ],
            compiler_params=pltpu.CompilerParams(
                collective_id=0, has_side_effects=True, vmem_limit_bytes=32 * 1024 * 1024
            ),
            cost_estimate=pl.CostEstimate(
                flops=16 * n * rows * rows * width,
                bytes_accessed=12 * rows * width,
                transcendentals=4 * n * rows * rows,
            ),
        )(image, text, scale, offset)

    return jax.shard_map(
        per_device,
        mesh=mesh,
        in_specs=(P(("outer", "inner"), None), P(("outer", "inner"), None), P(), P()),
        out_specs=(P(("outer", "inner"), None), P(("outer", "inner"), None)),
        check_vma=False,
    )
```

```python
import functools

import jax
import jax.numpy as jnp
from jax import lax
from jax.experimental import pallas as pl
from jax.experimental.pallas import tpu as pltpu
from jax.sharding import PartitionSpec as P

MESH = pl.DeviceIdType.MESH
TEXT, IMAGE = 0, 1
HALVES = 2


def kernel(
    n, m, image, text, scale, offset, grad_image, grad_text,
    own, group, guest, load_sem, line_send, line_recv, side_send, side_recv,
):
    outer, z = lax.axis_index("outer"), lax.axis_index("inner")
    above, below = lax.rem(outer + 1, m), lax.rem(outer + m - 1, m)
    rows = text.shape[0]
    source = (text, image)
    side = (above, below)

    loads = [pltpu.make_async_copy(source[k], own.at[k], load_sem.at[k]) for k in (TEXT, IMAGE)]
    for load in loads:
        load.start()

    barrier = pltpu.get_barrier_semaphore()

    def greet(o, i):
        pl.semaphore_signal(barrier, inc=1, device_id=(o, i), device_id_type=MESH)

    greet(above, z)
    greet(below, z)
    pl.when(z > 0)(lambda: greet(outer, z - 1))
    pl.when(z < n - 1)(lambda: greet(outer, z + 1))
    pl.semaphore_wait(barrier, 2 + (z > 0).astype(jnp.int32) + (z < n - 1).astype(jnp.int32))

    def along(k, src, slot, way):
        return pltpu.make_async_remote_copy(
            src_ref=src,
            dst_ref=group.at[k, slot],
            send_sem=line_send.at[k, slot, way],
            recv_sem=line_recv.at[k, slot],
            device_id=(outer, z + (1 if way else -1)),
            device_id_type=MESH,
        )

    def across(k, src, slot):
        return pltpu.make_async_remote_copy(
            src_ref=src,
            dst_ref=guest.at[k, slot],
            send_sem=side_send.at[k, slot],
            recv_sem=side_recv.at[k, slot],
            device_id=(side[k], z),
            device_id_type=MESH,
        )

    def has_next(way):
        return z < n - 1 if way else z > 0

    def add(k, block, first=False):
        out = (grad_image, grad_text)[k]
        product = lax.dot_general(
            own[1 - k], block[...], (((1,), (1,)), ((), ())), preferred_element_type=jnp.float32
        )
        logit = scale[0] * product + offset[0]
        if first:
            row = lax.broadcasted_iota(jnp.int32, (rows, rows), 0)
            column = lax.broadcasted_iota(jnp.int32, (rows, rows), 1)
            sign = jnp.where(row == column, 1.0, -1.0)
            coef = -sign * jax.nn.sigmoid(-sign * logit) * scale[0]
        else:
            coef = jax.nn.sigmoid(logit) * scale[0]
        term = jnp.dot(coef.astype(jnp.bfloat16), block[...], preferred_element_type=jnp.float32)
        out[...] = term if first else out[...] + term

    for k in (TEXT, IMAGE):
        for way in (1, 0):
            pl.when(has_next(way))(lambda: along(k, source[k], z, way).start())
        across(k, source[k], z).start()

    for load in loads:
        load.wait()
    for k in (TEXT, IMAGE):
        add(k, own.at[k], first=True)

    def visit(k, slot):
        across(k, guest.at[k, slot], slot).wait_recv()
        add(k, guest.at[k, slot])

    visit(TEXT, z)

    def step(s, _):
        def from_line(k):
            for way in (1, 0):
                slot = z - s if way else z + s

                @pl.when(slot >= 0 if way else slot < n)
                def _():
                    along(k, source[k], slot, way).wait_recv()
                    pl.when(has_next(way))(
                        lambda: along(k, group.at[k, slot], slot, way).start()
                    )
                    across(k, group.at[k, slot], slot).start()

            for way in (1, 0):
                slot = z - s if way else z + s
                pl.when(slot >= 0 if way else slot < n)(lambda: add(k, group.at[k, slot]))

        from_line(TEXT)
        pl.when(z - s + 1 >= 0)(lambda: visit(IMAGE, z - s + 1))
        pl.when((z + s - 1 < n) & (s > 1))(lambda: visit(IMAGE, z + s - 1))
        from_line(IMAGE)
        pl.when(z - s >= 0)(lambda: visit(TEXT, z - s))
        pl.when(z + s < n)(lambda: visit(TEXT, z + s))
        return 0

    lax.fori_loop(1, n, step, 0)
    if n > 1:
        pl.when(z - n + 1 >= 0)(lambda: visit(IMAGE, z - n + 1))
        pl.when(z + n - 1 < n)(lambda: visit(IMAGE, z + n - 1))

    def drain(slot, _):
        for k in (TEXT, IMAGE):
            across(k, source[k], slot).wait_send()
            pl.when((slot <= z) & (z < n - 1))(lambda: along(k, source[k], slot, 1).wait_send())
            pl.when((slot >= z) & (z > 0))(lambda: along(k, source[k], slot, 0).wait_send())
        return 0

    lax.fori_loop(0, n, drain, 0)


def line4_kernel(
    m, image, text, scale, offset, grad_image, grad_text,
    mine, group, guest, images, guest_images, total, part_out, part_in, row_out, row_in,
    load_sem, line_send, line_recv, side_send, side_recv, image_send, image_recv,
    guest_send, guest_recv, part_send, part_recv, row_send, row_recv,
):
    outer, z = lax.axis_index("outer"), lax.axis_index("inner")
    above, below = lax.rem(outer + 1, m), lax.rem(outer + m - 1, m)
    rows = text.shape[0]
    half = rows // HALVES
    is_end = (z == 0) | (z == 3)
    is_middle = (z == 1) | (z == 2)
    high = (z >= 2).astype(jnp.int32)
    end, middle = 3 * high, 1 + high
    far_end, far_middle = 3 - end, 3 - middle

    loads = [
        pltpu.make_async_copy(image, images.at[0], load_sem.at[0]),
        pltpu.make_async_copy(text, mine, load_sem.at[1]),
    ]
    for load in loads:
        load.start()

    barrier = pltpu.get_barrier_semaphore()

    def greet(o, i):
        pl.semaphore_signal(barrier, inc=1, device_id=(o, i), device_id_type=MESH)

    greet(above, z)
    greet(below, z)
    pl.when(z > 0)(lambda: greet(outer, z - 1))
    pl.when(z < 3)(lambda: greet(outer, z + 1))
    pl.semaphore_wait(barrier, 2 + (z > 0).astype(jnp.int32) + (z < 3).astype(jnp.int32))

    def remote(src, dst, send, recv, o, i):
        return pltpu.make_async_remote_copy(
            src_ref=src, dst_ref=dst, send_sem=send, recv_sem=recv,
            device_id=(o, i), device_id_type=MESH,
        )

    def along(src, slot, way, to):
        return remote(src, group.at[slot], line_send.at[slot, way], line_recv.at[slot], outer, to)

    def across(src, slot):
        return remote(src, guest.at[slot], side_send.at[slot], side_recv.at[slot], above, z)

    def image_inward():
        return remote(image, images.at[1], image_send.at[0], image_recv.at[0], outer, middle)

    def image_across(src, i):
        return remote(src, guest_images.at[i], guest_send.at[i], guest_recv.at[i], below, z)

    def part(i, h):
        rows_h = pl.ds(h * half, half)
        return remote(
            part_out.at[i, rows_h], part_in.at[i, rows_h],
            part_send.at[i, h], part_recv.at[i, h], outer, far_middle,
        )

    def row_block(h):
        rows_h = pl.ds(h * half, half)
        return remote(
            row_out.at[rows_h], row_in.at[rows_h], row_send.at[h], row_recv.at[h], outer, end
        )

    def pair(left, right, positive):
        product = lax.dot_general(
            left, right[...], (((1,), (1,)), ((), ())), preferred_element_type=jnp.float32
        )
        logit = scale[0] * product + offset[0]
        if positive:
            row = lax.broadcasted_iota(jnp.int32, (rows, rows), 0)
            column = lax.broadcasted_iota(jnp.int32, (rows, rows), 1)
            sign = jnp.where(row == column, 1.0, -1.0)
            coef = -sign * jax.nn.sigmoid(-sign * logit) * scale[0]
        else:
            coef = jax.nn.sigmoid(logit) * scale[0]
        return jnp.dot(coef.astype(jnp.bfloat16), right[...], preferred_element_type=jnp.float32)

    def add_image(block, positive=False, first=False):
        term = pair(images[0], block, positive)
        grad_image[...] = term if first else grad_image[...] + term

    def add_text(i, left, block, positive=False, first=False):
        term = pair(left[...], block, positive)
        total[i] = term if first else total[i] + term

    def arrive(slot):
        along(text, slot, 0, end).wait_recv()

    def visit(slot):
        across(text, slot).wait_recv()
        add_image(guest.at[slot])

    @pl.when(is_end)
    def _():
        along(text, z, 0, middle).start()
        image_inward().start()
        across(text, z).start()
        for load in loads:
            load.wait()
        add_image(mine, positive=True, first=True)
        visit(z)
        for slot, previous in ((middle, None), (far_middle, middle), (far_end, far_middle)):
            arrive(slot)
            across(group.at[slot], slot).start()
            add_image(group.at[slot])
            if previous is not None:
                visit(previous)
        visit(far_end)
        for h in range(HALVES):
            row_block(h).wait_recv()
            rows_h = pl.ds(h * half, half)
            grad_text[rows_h, :] = row_in[rows_h, :].astype(jnp.float32)
        along(text, z, 0, middle).wait_send()
        image_inward().wait_send()

    @pl.when(is_middle)
    def _():
        along(text, z, 0, far_middle).start()
        along(text, z, 1, end).start()
        image_across(image, 0).start()
        across(text, z).start()
        for load in loads:
            load.wait()
        add_image(mine, positive=True, first=True)
        add_text(0, mine, images.at[0], positive=True, first=True)
        image_across(image, 0).wait_recv()
        add_text(0, mine, guest_images.at[0])

        arrive(end)
        along(group.at[end], end, 0, far_middle).start()
        across(group.at[end], end).start()
        add_text(1, group.at[end], images.at[0], first=True)
        arrive(far_middle)
        along(group.at[far_middle], far_middle, 0, end).start()
        across(group.at[far_middle], far_middle).start()
        add_text(2, group.at[far_middle], images.at[0], first=True)
        add_text(2, group.at[far_middle], guest_images.at[0])

        image_inward().wait_recv()
        image_across(images.at[1], 1).start()
        arrive(far_end)
        along(group.at[far_end], far_end, 0, end).start()
        across(group.at[far_end], far_end).start()
        add_text(3, group.at[far_end], images.at[0], first=True)
        add_text(3, group.at[far_end], guest_images.at[0])
        add_text(3, group.at[far_end], images.at[1])
        add_text(2, group.at[far_middle], images.at[1])
        image_across(image, 1).wait_recv()
        for i, slot, to in ((3, far_end, 1), (2, far_middle, 0)):
            add_text(i, group.at[slot], guest_images.at[1])
            part_out[to] = total[i].astype(jnp.bfloat16)
            for h in range(HALVES):
                part(to, h).start()

        add_text(1, group.at[end], guest_images.at[0])
        add_text(1, group.at[end], images.at[1], positive=True)
        add_text(1, group.at[end], guest_images.at[1])
        for h in range(HALVES):
            part(1, h).wait_recv()
            rows_h = pl.ds(h * half, half)
            row_out[rows_h, :] = (
                total[1, rows_h, :] + part_in[1, rows_h, :].astype(jnp.float32)
            ).astype(jnp.bfloat16)
            row_block(h).start()
        add_text(0, mine, images.at[1])
        add_text(0, mine, guest_images.at[1])
        for slot in (end, far_middle, far_end):
            add_image(group.at[slot])
        for slot in (z, end, far_middle, far_end):
            visit(slot)
        for h in range(HALVES):
            part(0, h).wait_recv()
            rows_h = pl.ds(h * half, half)
            grad_text[rows_h, :] = total[0, rows_h, :] + part_in[0, rows_h, :].astype(jnp.float32)

        along(text, z, 0, far_middle).wait_send()
        along(text, z, 1, end).wait_send()
        along(text, end, 0, far_middle).wait_send()
        along(text, far_middle, 0, end).wait_send()
        along(text, far_end, 0, end).wait_send()
        for i in (0, 1):
            image_across(image, i).wait_send()
            for h in range(HALVES):
                part(i, h).wait_send()
        for h in range(HALVES):
            row_block(h).wait_send()

    for slot in range(4):
        across(text, slot).wait_send()


def solution(mesh):
    n, m = mesh.shape["inner"], mesh.shape["outer"]

    def per_device(image, text, scale, offset):
        rows, width = image.shape
        dma = pltpu.SemaphoreType.DMA
        block = (rows, width)
        if n == 4:
            body = functools.partial(line4_kernel, m)
            scratch = [
                pltpu.VMEM(block, jnp.bfloat16),
                pltpu.VMEM((4, *block), jnp.bfloat16),
                pltpu.VMEM((4, *block), jnp.bfloat16),
                pltpu.VMEM((2, *block), jnp.bfloat16),
                pltpu.VMEM((2, *block), jnp.bfloat16),
                pltpu.VMEM((4, *block), jnp.float32),
                pltpu.VMEM((2, *block), jnp.bfloat16),
                pltpu.VMEM((2, *block), jnp.bfloat16),
                pltpu.VMEM(block, jnp.bfloat16),
                pltpu.VMEM(block, jnp.bfloat16),
                dma((2,)), dma((4, 2)), dma((4,)), dma((4,)), dma((4,)),
                dma((1,)), dma((1,)), dma((2,)), dma((2,)),
                dma((2, HALVES)), dma((2, HALVES)), dma((HALVES,)), dma((HALVES,)),
            ]
        else:
            body = functools.partial(kernel, n, m)
            scratch = [
                pltpu.VMEM((2, *block), jnp.bfloat16),
                pltpu.VMEM((2, n, *block), jnp.bfloat16),
                pltpu.VMEM((2, n, *block), jnp.bfloat16),
                dma((2,)), dma((2, n, 2)), dma((2, n)), dma((2, n)), dma((2, n)),
            ]
        return pl.pallas_call(
            body,
            out_shape=(jax.ShapeDtypeStruct((rows, width), jnp.float32),) * 2,
            in_specs=[pl.BlockSpec(memory_space=pl.ANY)] * 2
            + [pl.BlockSpec(memory_space=pltpu.SMEM)] * 2,
            out_specs=(pl.BlockSpec(memory_space=pltpu.VMEM),) * 2,
            scratch_shapes=scratch,
            compiler_params=pltpu.CompilerParams(
                collective_id=0, has_side_effects=True, vmem_limit_bytes=60 * 1024 * 1024
            ),
            cost_estimate=pl.CostEstimate(
                flops=16 * n * rows * rows * width,
                bytes_accessed=12 * rows * width,
                transcendentals=4 * n * rows * rows,
            ),
        )(image, text, scale, offset)

    return jax.shard_map(
        per_device,
        mesh=mesh,
        in_specs=(P(("outer", "inner"), None), P(("outer", "inner"), None), P(), P()),
        out_specs=(P(("outer", "inner"), None), P(("outer", "inner"), None)),
        check_vma=False,
    )
```

```python
import functools

import jax
import jax.numpy as jnp
from jax import lax
from jax.experimental import pallas as pl
from jax.experimental.pallas import tpu as pltpu
from jax.sharding import PartitionSpec as P

MESH = pl.DeviceIdType.MESH
TEXT, IMAGE = 0, 1
CHUNKS = 4


def kernel(
    n, m, image, text, scale, offset, grad_image, grad_text,
    own, group, guest, load_sem, line_send, line_recv, side_send, side_recv,
):
    outer, z = lax.axis_index("outer"), lax.axis_index("inner")
    above, below = lax.rem(outer + 1, m), lax.rem(outer + m - 1, m)
    rows = text.shape[0]
    source = (text, image)
    side = (above, below)

    loads = [pltpu.make_async_copy(source[k], own.at[k], load_sem.at[k]) for k in (TEXT, IMAGE)]
    for load in loads:
        load.start()

    barrier = pltpu.get_barrier_semaphore()

    def greet(o, i):
        pl.semaphore_signal(barrier, inc=1, device_id=(o, i), device_id_type=MESH)

    greet(above, z)
    greet(below, z)
    pl.when(z > 0)(lambda: greet(outer, z - 1))
    pl.when(z < n - 1)(lambda: greet(outer, z + 1))
    pl.semaphore_wait(barrier, 2 + (z > 0).astype(jnp.int32) + (z < n - 1).astype(jnp.int32))

    def along(k, src, slot, way):
        return pltpu.make_async_remote_copy(
            src_ref=src,
            dst_ref=group.at[k, slot],
            send_sem=line_send.at[k, slot, way],
            recv_sem=line_recv.at[k, slot],
            device_id=(outer, z + (1 if way else -1)),
            device_id_type=MESH,
        )

    def across(k, src, slot):
        return pltpu.make_async_remote_copy(
            src_ref=src,
            dst_ref=guest.at[k, slot],
            send_sem=side_send.at[k, slot],
            recv_sem=side_recv.at[k, slot],
            device_id=(side[k], z),
            device_id_type=MESH,
        )

    def has_next(way):
        return z < n - 1 if way else z > 0

    def add(k, block, first=False):
        out = (grad_image, grad_text)[k]
        product = lax.dot_general(
            own[1 - k], block[...], (((1,), (1,)), ((), ())), preferred_element_type=jnp.float32
        )
        logit = scale[0] * product + offset[0]
        if first:
            row = lax.broadcasted_iota(jnp.int32, (rows, rows), 0)
            column = lax.broadcasted_iota(jnp.int32, (rows, rows), 1)
            sign = jnp.where(row == column, 1.0, -1.0)
            coef = -sign * jax.nn.sigmoid(-sign * logit) * scale[0]
        else:
            coef = jax.nn.sigmoid(logit) * scale[0]
        term = jnp.dot(coef.astype(jnp.bfloat16), block[...], preferred_element_type=jnp.float32)
        out[...] = term if first else out[...] + term

    for k in (TEXT, IMAGE):
        for way in (1, 0):
            pl.when(has_next(way))(lambda: along(k, source[k], z, way).start())
        across(k, source[k], z).start()

    for load in loads:
        load.wait()
    for k in (TEXT, IMAGE):
        add(k, own.at[k], first=True)

    def visit(k, slot):
        across(k, guest.at[k, slot], slot).wait_recv()
        add(k, guest.at[k, slot])

    visit(TEXT, z)

    def step(s, _):
        def from_line(k):
            for way in (1, 0):
                slot = z - s if way else z + s

                @pl.when(slot >= 0 if way else slot < n)
                def _():
                    along(k, source[k], slot, way).wait_recv()
                    pl.when(has_next(way))(
                        lambda: along(k, group.at[k, slot], slot, way).start()
                    )
                    across(k, group.at[k, slot], slot).start()

            for way in (1, 0):
                slot = z - s if way else z + s
                pl.when(slot >= 0 if way else slot < n)(lambda: add(k, group.at[k, slot]))

        from_line(TEXT)
        pl.when(z - s + 1 >= 0)(lambda: visit(IMAGE, z - s + 1))
        pl.when((z + s - 1 < n) & (s > 1))(lambda: visit(IMAGE, z + s - 1))
        from_line(IMAGE)
        pl.when(z - s >= 0)(lambda: visit(TEXT, z - s))
        pl.when(z + s < n)(lambda: visit(TEXT, z + s))
        return 0

    lax.fori_loop(1, n, step, 0)
    if n > 1:
        pl.when(z - n + 1 >= 0)(lambda: visit(IMAGE, z - n + 1))
        pl.when(z + n - 1 < n)(lambda: visit(IMAGE, z + n - 1))

    def drain(slot, _):
        for k in (TEXT, IMAGE):
            across(k, source[k], slot).wait_send()
            pl.when((slot <= z) & (z < n - 1))(lambda: along(k, source[k], slot, 1).wait_send())
            pl.when((slot >= z) & (z > 0))(lambda: along(k, source[k], slot, 0).wait_send())
        return 0

    lax.fori_loop(0, n, drain, 0)


def line4_kernel(
    m, image, text, scale, offset, grad_image, grad_text,
    mine, group, guest, images, guest_images, total, part_out, part_in, row_out, row_in,
    load_sem, line_send, line_recv, side_send, side_recv, image_send, image_recv,
    guest_send, guest_recv, part_send, part_recv, row_send, row_recv,
):
    outer, z = lax.axis_index("outer"), lax.axis_index("inner")
    above, below = lax.rem(outer + 1, m), lax.rem(outer + m - 1, m)
    rows = text.shape[0]
    size = rows // CHUNKS
    is_end = (z == 0) | (z == 3)
    is_middle = (z == 1) | (z == 2)
    high = (z >= 2).astype(jnp.int32)
    end, middle = 3 * high, 1 + high
    far_end, far_middle = 3 - end, 3 - middle

    loads = [
        pltpu.make_async_copy(image, images.at[0], load_sem.at[0]),
        pltpu.make_async_copy(text, mine, load_sem.at[1]),
    ]
    for load in loads:
        load.start()

    barrier = pltpu.get_barrier_semaphore()

    def greet(o, i):
        pl.semaphore_signal(barrier, inc=1, device_id=(o, i), device_id_type=MESH)

    greet(above, z)
    greet(below, z)
    pl.when(z > 0)(lambda: greet(outer, z - 1))
    pl.when(z < 3)(lambda: greet(outer, z + 1))
    pl.semaphore_wait(barrier, 2 + (z > 0).astype(jnp.int32) + (z < 3).astype(jnp.int32))

    def remote(src, dst, send, recv, o, i):
        return pltpu.make_async_remote_copy(
            src_ref=src, dst_ref=dst, send_sem=send, recv_sem=recv,
            device_id=(o, i), device_id_type=MESH,
        )

    def piece(c):
        return pl.ds(c * size, size)

    def along(src, slot, way, to, c):
        return remote(
            src.at[piece(c)], group.at[slot, piece(c)],
            line_send.at[slot, way, c], line_recv.at[slot, c], outer, to,
        )

    def across(src, slot):
        return remote(src, guest.at[slot], side_send.at[slot], side_recv.at[slot], above, z)

    def image_inward(c):
        return remote(
            image.at[piece(c)], images.at[1, piece(c)],
            image_send.at[c], image_recv.at[c], outer, middle,
        )

    def image_across(src, i, c):
        return remote(
            src.at[piece(c)], guest_images.at[i, piece(c)],
            guest_send.at[i, c], guest_recv.at[i, c], below, z,
        )

    def part(i, c):
        return remote(
            part_out.at[i, piece(c)], part_in.at[i, piece(c)],
            part_send.at[i, c], part_recv.at[i, c], outer, far_middle,
        )

    def row_block(c):
        return remote(
            row_out.at[piece(c)], row_in.at[piece(c)], row_send.at[c], row_recv.at[c], outer, end
        )

    def pair(left, right, positive):
        product = lax.dot_general(
            left, right[...], (((1,), (1,)), ((), ())), preferred_element_type=jnp.float32
        )
        logit = scale[0] * product + offset[0]
        if positive:
            row = lax.broadcasted_iota(jnp.int32, (rows, rows), 0)
            column = lax.broadcasted_iota(jnp.int32, (rows, rows), 1)
            sign = jnp.where(row == column, 1.0, -1.0)
            coef = -sign * jax.nn.sigmoid(-sign * logit) * scale[0]
        else:
            coef = jax.nn.sigmoid(logit) * scale[0]
        return jnp.dot(coef.astype(jnp.bfloat16), right[...], preferred_element_type=jnp.float32)

    def add_image(block, positive=False, first=False):
        term = pair(images[0], block, positive)
        grad_image[...] = term if first else grad_image[...] + term

    def add_text(i, left, block, positive=False, first=False):
        term = pair(left[...], block, positive)
        total[i] = term if first else total[i] + term

    def visit(slot):
        across(text, slot).wait_recv()
        add_image(guest.at[slot])

    chunks = range(CHUNKS)

    @pl.when(is_end)
    def _():
        for c in chunks:
            along(text, z, 0, middle, c).start()
        across(text, z).start()
        for load in loads:
            load.wait()
        for c in chunks[:-1]:
            along(text, z, 0, middle, c).wait_send()
        for c in chunks:
            image_inward(c).start()
        add_image(mine, positive=True, first=True)
        visit(z)
        for slot, previous in ((middle, None), (far_middle, middle), (far_end, far_middle)):
            for c in chunks:
                along(text, slot, 0, end, c).wait_recv()
            across(group.at[slot], slot).start()
            add_image(group.at[slot])
            if previous is not None:
                visit(previous)
        visit(far_end)
        for c in chunks:
            row_block(c).wait_recv()
            grad_text[piece(c), :] = row_in[piece(c), :].astype(jnp.float32)
        along(text, z, 0, middle, CHUNKS - 1).wait_send()
        for c in chunks:
            image_inward(c).wait_send()

    @pl.when(is_middle)
    def _():
        own, beside, over, far = mine, group.at[end], group.at[far_middle], group.at[far_end]
        for c in chunks:
            along(text, z, 0, far_middle, c).start()
        for c in chunks:
            along(text, z, 1, end, c).start()
        for c in chunks:
            image_across(image, 0, c).start()
        across(text, z).start()
        for load in loads:
            load.wait()
        add_image(own, positive=True, first=True)
        for c in chunks:
            along(text, end, 0, middle, c).wait_recv()
            along(beside, end, 0, far_middle, c).start()
        add_text(0, own, images.at[0], positive=True, first=True)
        add_text(1, beside, images.at[0], first=True)
        for c in chunks:
            along(text, far_middle, 0, middle, c).wait_recv()
            along(over, far_middle, 0, end, c).start()
        across(beside, end).start()
        add_text(2, over, images.at[0], first=True)
        for c in chunks:
            image_across(image, 0, c).wait_recv()
        early = (
            lambda: add_text(2, over, guest_images.at[0]),
            lambda: add_text(1, beside, guest_images.at[0]),
            lambda: add_text(0, own, guest_images.at[0]),
            lambda: add_image(beside),
        )
        for c in chunks:
            early[c]()
            image_inward(c).wait_recv()
            image_across(images.at[1], 1, c).start()
            along(text, far_end, 0, middle, c).wait_recv()
            along(far, far_end, 0, end, c).start()
        across(over, far_middle).start()
        add_text(3, far, images.at[0], first=True)
        add_text(3, far, guest_images.at[0])
        add_text(3, far, images.at[1])
        add_text(2, over, images.at[1])
        for c in chunks:
            image_across(image, 1, c).wait_recv()
        add_text(3, far, guest_images.at[1])
        for c in chunks:
            part_out[1, piece(c), :] = total[3, piece(c), :].astype(jnp.bfloat16)
            part(1, c).start()
        across(far, far_end).start()
        add_text(2, over, guest_images.at[1])
        part_out[0] = total[2].astype(jnp.bfloat16)
        add_text(1, beside, images.at[1], positive=True)
        add_text(1, beside, guest_images.at[1])
        for c in chunks[:-1]:
            part(1, c).wait_send()
        for c in chunks:
            part(0, c).start()
        late = (
            lambda: add_image(over),
            lambda: add_image(far),
            lambda: visit(z),
            lambda: visit(end),
        )
        for c in chunks:
            part(1, c).wait_recv()
            row_out[piece(c), :] = (
                total[1, piece(c), :] + part_in[1, piece(c), :].astype(jnp.float32)
            ).astype(jnp.bfloat16)
            row_block(c).start()
            late[c]()
        add_text(0, own, images.at[1])
        add_text(0, own, guest_images.at[1])
        visit(far_middle)
        visit(far_end)
        for c in chunks:
            part(0, c).wait_recv()
            grad_text[piece(c), :] = (
                total[0, piece(c), :] + part_in[0, piece(c), :].astype(jnp.float32)
            )

        part(1, CHUNKS - 1).wait_send()
        for c in chunks:
            along(text, z, 0, far_middle, c).wait_send()
            along(text, z, 1, end, c).wait_send()
            along(text, end, 0, far_middle, c).wait_send()
            along(text, far_middle, 0, end, c).wait_send()
            along(text, far_end, 0, end, c).wait_send()
            image_across(image, 0, c).wait_send()
            image_across(image, 1, c).wait_send()
            part(0, c).wait_send()
            row_block(c).wait_send()

    for slot in range(4):
        across(text, slot).wait_send()


def solution(mesh):
    n, m = mesh.shape["inner"], mesh.shape["outer"]

    def per_device(image, text, scale, offset):
        rows, width = image.shape
        dma = pltpu.SemaphoreType.DMA
        block = (rows, width)
        if n == 4:
            body = functools.partial(line4_kernel, m)
            scratch = [
                pltpu.VMEM(block, jnp.bfloat16),
                pltpu.VMEM((4, *block), jnp.bfloat16),
                pltpu.VMEM((4, *block), jnp.bfloat16),
                pltpu.VMEM((2, *block), jnp.bfloat16),
                pltpu.VMEM((2, *block), jnp.bfloat16),
                pltpu.VMEM((4, *block), jnp.float32),
                pltpu.VMEM((2, *block), jnp.bfloat16),
                pltpu.VMEM((2, *block), jnp.bfloat16),
                pltpu.VMEM(block, jnp.bfloat16),
                pltpu.VMEM(block, jnp.bfloat16),
                dma((2,)), dma((4, 2, CHUNKS)), dma((4, CHUNKS)), dma((4,)), dma((4,)),
                dma((CHUNKS,)), dma((CHUNKS,)), dma((2, CHUNKS)), dma((2, CHUNKS)),
                dma((2, CHUNKS)), dma((2, CHUNKS)), dma((CHUNKS,)), dma((CHUNKS,)),
            ]
        else:
            body = functools.partial(kernel, n, m)
            scratch = [
                pltpu.VMEM((2, *block), jnp.bfloat16),
                pltpu.VMEM((2, n, *block), jnp.bfloat16),
                pltpu.VMEM((2, n, *block), jnp.bfloat16),
                dma((2,)), dma((2, n, 2)), dma((2, n)), dma((2, n)), dma((2, n)),
            ]
        return pl.pallas_call(
            body,
            out_shape=(pltpu.VMEM((rows, width), jnp.float32),) * 2,
            in_specs=[pl.BlockSpec(memory_space=pltpu.HBM)] * 2
            + [pl.BlockSpec(memory_space=pltpu.SMEM)] * 2,
            out_specs=(pl.BlockSpec(memory_space=pltpu.VMEM),) * 2,
            scratch_shapes=scratch,
            compiler_params=pltpu.CompilerParams(
                collective_id=0, has_side_effects=True, vmem_limit_bytes=32 * 1024 * 1024
            ),
            cost_estimate=pl.CostEstimate(
                flops=16 * n * rows * rows * width,
                bytes_accessed=12 * rows * width,
                transcendentals=4 * n * rows * rows,
            ),
        )(image, text, scale, offset)

    return jax.shard_map(
        per_device,
        mesh=mesh,
        in_specs=(P(("outer", "inner"), None), P(("outer", "inner"), None), P(), P()),
        out_specs=(P(("outer", "inner"), None), P(("outer", "inner"), None)),
        check_vma=False,
    )
```

```python
import functools

import jax
import jax.numpy as jnp
from jax import lax
from jax.experimental import pallas as pl
from jax.experimental.pallas import tpu as pltpu
from jax.sharding import PartitionSpec as P

MESH = pl.DeviceIdType.MESH
TEXT, IMAGE = 0, 1
CHUNKS = 4


def kernel(
    n, m, image, text, scale, offset, grad_image, grad_text,
    own, group, guest, load_sem, line_send, line_recv, side_send, side_recv,
):
    outer, z = lax.axis_index("outer"), lax.axis_index("inner")
    above, below = lax.rem(outer + 1, m), lax.rem(outer + m - 1, m)
    rows = text.shape[0]
    source = (text, image)
    side = (above, below)

    loads = [pltpu.make_async_copy(source[k], own.at[k], load_sem.at[k]) for k in (TEXT, IMAGE)]
    for load in loads:
        load.start()

    barrier = pltpu.get_barrier_semaphore()

    def greet(o, i):
        pl.semaphore_signal(barrier, inc=1, device_id=(o, i), device_id_type=MESH)

    greet(above, z)
    greet(below, z)
    pl.when(z > 0)(lambda: greet(outer, z - 1))
    pl.when(z < n - 1)(lambda: greet(outer, z + 1))
    pl.semaphore_wait(barrier, 2 + (z > 0).astype(jnp.int32) + (z < n - 1).astype(jnp.int32))

    def along(k, src, slot, way):
        return pltpu.make_async_remote_copy(
            src_ref=src,
            dst_ref=group.at[k, slot],
            send_sem=line_send.at[k, slot, way],
            recv_sem=line_recv.at[k, slot],
            device_id=(outer, z + (1 if way else -1)),
            device_id_type=MESH,
        )

    def across(k, src, slot):
        return pltpu.make_async_remote_copy(
            src_ref=src,
            dst_ref=guest.at[k, slot],
            send_sem=side_send.at[k, slot],
            recv_sem=side_recv.at[k, slot],
            device_id=(side[k], z),
            device_id_type=MESH,
        )

    def has_next(way):
        return z < n - 1 if way else z > 0

    def add(k, block, first=False):
        out = (grad_image, grad_text)[k]
        product = lax.dot_general(
            own[1 - k], block[...], (((1,), (1,)), ((), ())), preferred_element_type=jnp.float32
        )
        logit = scale[0] * product + offset[0]
        if first:
            row = lax.broadcasted_iota(jnp.int32, (rows, rows), 0)
            column = lax.broadcasted_iota(jnp.int32, (rows, rows), 1)
            sign = jnp.where(row == column, 1.0, -1.0)
            coef = -sign * jax.nn.sigmoid(-sign * logit) * scale[0]
        else:
            coef = jax.nn.sigmoid(logit) * scale[0]
        term = jnp.dot(coef.astype(jnp.bfloat16), block[...], preferred_element_type=jnp.float32)
        out[...] = term if first else out[...] + term

    for k in (TEXT, IMAGE):
        for way in (1, 0):
            pl.when(has_next(way))(lambda: along(k, source[k], z, way).start())
        across(k, source[k], z).start()

    for load in loads:
        load.wait()
    for k in (TEXT, IMAGE):
        add(k, own.at[k], first=True)

    def visit(k, slot):
        across(k, guest.at[k, slot], slot).wait_recv()
        add(k, guest.at[k, slot])

    visit(TEXT, z)

    def step(s, _):
        def from_line(k):
            for way in (1, 0):
                slot = z - s if way else z + s

                @pl.when(slot >= 0 if way else slot < n)
                def _():
                    along(k, source[k], slot, way).wait_recv()
                    pl.when(has_next(way))(
                        lambda: along(k, group.at[k, slot], slot, way).start()
                    )
                    across(k, group.at[k, slot], slot).start()

            for way in (1, 0):
                slot = z - s if way else z + s
                pl.when(slot >= 0 if way else slot < n)(lambda: add(k, group.at[k, slot]))

        from_line(TEXT)
        pl.when(z - s + 1 >= 0)(lambda: visit(IMAGE, z - s + 1))
        pl.when((z + s - 1 < n) & (s > 1))(lambda: visit(IMAGE, z + s - 1))
        from_line(IMAGE)
        pl.when(z - s >= 0)(lambda: visit(TEXT, z - s))
        pl.when(z + s < n)(lambda: visit(TEXT, z + s))
        return 0

    lax.fori_loop(1, n, step, 0)
    if n > 1:
        pl.when(z - n + 1 >= 0)(lambda: visit(IMAGE, z - n + 1))
        pl.when(z + n - 1 < n)(lambda: visit(IMAGE, z + n - 1))

    def drain(slot, _):
        for k in (TEXT, IMAGE):
            across(k, source[k], slot).wait_send()
            pl.when((slot <= z) & (z < n - 1))(lambda: along(k, source[k], slot, 1).wait_send())
            pl.when((slot >= z) & (z > 0))(lambda: along(k, source[k], slot, 0).wait_send())
        return 0

    lax.fori_loop(0, n, drain, 0)


def line4_kernel(
    m, image, text, scale, offset, grad_image, grad_text,
    group, guest, images, total, part_out, part_in, row_out, row_in,
    load_sem, line_send, line_recv, side_send, side_recv, image_send, image_recv,
    guest_send, guest_recv, part_send, part_recv, row_send, row_recv, turn,
):
    outer, z = lax.axis_index("outer"), lax.axis_index("inner")
    above, below = lax.rem(outer + 1, m), lax.rem(outer + m - 1, m)
    rows, width = text.shape
    size = rows // CHUNKS
    is_end = (z == 0) | (z == 3)
    is_middle = (z == 1) | (z == 2)
    high = (z >= 2).astype(jnp.int32)
    end, middle = 3 * high, 1 + high
    far_end, far_middle = 3 - end, 3 - middle

    loads = [
        pltpu.make_async_copy(image, images.at[0], load_sem.at[0]),
        pltpu.make_async_copy(text, group.at[z], load_sem.at[1]),
    ]
    for load in loads:
        load.start()

    barrier = pltpu.get_barrier_semaphore()

    def greet(o, i):
        pl.semaphore_signal(barrier, inc=1, device_id=(o, i), device_id_type=MESH)

    greet(above, z)
    greet(below, z)
    pl.when(z > 0)(lambda: greet(outer, z - 1))
    pl.when(z < 3)(lambda: greet(outer, z + 1))
    pl.semaphore_wait(barrier, 2 + (z > 0).astype(jnp.int32) + (z < 3).astype(jnp.int32))

    def remote(src, dst, send, recv, o, i):
        return pltpu.make_async_remote_copy(
            src_ref=src, dst_ref=dst, send_sem=send, recv_sem=recv,
            device_id=(o, i), device_id_type=MESH,
        )

    def piece(c):
        return pl.ds(c * size, size)

    def along(src, slot, way, to, c):
        return remote(
            src.at[piece(c)], group.at[slot, piece(c)],
            line_send.at[slot, way, c], line_recv.at[slot, c], outer, to,
        )

    def across(src, slot):
        return remote(src, guest.at[slot], side_send.at[slot], side_recv.at[slot], above, z)

    def image_inward(c):
        return remote(
            image.at[piece(c)], images.at[1, piece(c)],
            image_send.at[c], image_recv.at[c], outer, middle,
        )

    def image_across(src, i, c):
        return remote(
            src.at[piece(c)], images.at[2 + i, piece(c)],
            guest_send.at[i, c], guest_recv.at[i, c], below, z,
        )

    def part(i, c):
        return remote(
            part_out.at[i, piece(c)], part_in.at[i, piece(c)],
            part_send.at[i, c], part_recv.at[i, c], outer, far_middle,
        )

    def row_block(c):
        return remote(
            row_out.at[piece(c)], row_in.at[piece(c)], row_send.at[c], row_recv.at[c], outer, end
        )

    def pair(left, blocks, match=None):
        right = blocks[...].reshape(-1, width)
        product = lax.dot_general(
            left, right, (((1,), (1,)), ((), ())), preferred_element_type=jnp.float32
        )
        logit = scale[0] * product + offset[0]
        if match is not None:
            row = lax.broadcasted_iota(jnp.int32, logit.shape, 0)
            column = lax.broadcasted_iota(jnp.int32, logit.shape, 1)
            sign = jnp.where(column == row + match, 1.0, -1.0)
            coef = -sign * jax.nn.sigmoid(-sign * logit) * scale[0]
        else:
            coef = jax.nn.sigmoid(logit) * scale[0]
        return jnp.dot(coef.astype(jnp.bfloat16), right, preferred_element_type=jnp.float32)

    def add_group():
        grad_image[...] = pair(images[0], group, z * rows)

    def add_guest():
        for slot in range(4):
            across(text, slot).wait_recv()
        grad_image[...] += pair(images[0], guest)

    chunks = range(CHUNKS)

    @pl.when(is_end)
    def _():
        for c in chunks:
            along(text, z, 0, middle, c).start()
        across(text, z).start()
        for c in chunks[:-1]:
            along(text, z, 0, middle, c).wait_send()
        odd = lax.rem(outer, 2) == 1
        pl.when(odd)(lambda: pl.semaphore_wait(turn, 1))
        for c in chunks:
            image_inward(c).start()
        for c in chunks[:-1]:
            image_inward(c).wait_send()
        pl.when(jnp.logical_not(odd) & (outer + 1 < m))(
            lambda: pl.semaphore_signal(
                turn, inc=1, device_id=(above, z), device_id_type=MESH
            )
        )
        for load in loads:
            load.wait()
        for slot in (middle, far_middle, far_end):
            for c in chunks:
                along(text, slot, 0, end, c).wait_recv()
            across(group.at[slot], slot).start()
        add_group()
        add_guest()
        for c in chunks:
            row_block(c).wait_recv()
            grad_text[piece(c), :] = row_in[piece(c), :].astype(jnp.float32)
        along(text, z, 0, middle, CHUNKS - 1).wait_send()
        image_inward(CHUNKS - 1).wait_send()

    @pl.when(is_middle)
    def _():
        beside, over, far = group.at[end], group.at[far_middle], group.at[far_end]
        for c in chunks:
            along(text, z, 0, far_middle, c).start()
            along(text, z, 1, end, c).start()
        for c in chunks:
            image_across(image, 0, c).start()
        across(text, z).start()
        for load in loads:
            load.wait()
        for c in chunks:
            along(text, end, 0, middle, c).wait_recv()
            along(beside, end, 0, far_middle, c).start()
        across(beside, end).start()
        for c in chunks:
            along(text, far_middle, 0, middle, c).wait_recv()
            along(over, far_middle, 0, end, c).start()
        across(over, far_middle).start()
        for c in chunks:
            image_inward(c).wait_recv()
            image_across(images.at[1], 1, c).start()
        for c in chunks:
            along(text, far_end, 0, middle, c).wait_recv()
            along(far, far_end, 0, end, c).start()
        for c in chunks:
            image_across(image, 0, c).wait_recv()
            image_across(image, 1, c).wait_recv()
        part_out[1] = pair(far[...], images).astype(jnp.bfloat16)
        for c in chunks:
            part(1, c).start()
        across(far, far_end).start()
        part_out[0] = pair(over[...], images).astype(jnp.bfloat16)
        total[1] = pair(beside[...], images, rows)
        add_group()
        for c in chunks:
            part(1, c).wait_recv()
            row_out[piece(c), :] = (
                total[1, piece(c), :] + part_in[1, piece(c), :].astype(jnp.float32)
            ).astype(jnp.bfloat16)
            row_block(c).start()
            if c == CHUNKS - 2:
                for early in chunks[:-1]:
                    part(1, early).wait_send()
                for late in chunks:
                    part(0, late).start()
        total[0] = pair(group[z], images, 0)
        add_guest()
        for c in chunks:
            part(0, c).wait_recv()
            grad_text[piece(c), :] = (
                total[0, piece(c), :] + part_in[0, piece(c), :].astype(jnp.float32)
            )

        part(1, CHUNKS - 1).wait_send()
        for c in chunks:
            along(text, z, 0, far_middle, c).wait_send()
            along(text, z, 1, end, c).wait_send()
            along(text, end, 0, far_middle, c).wait_send()
            along(text, far_middle, 0, end, c).wait_send()
            along(text, far_end, 0, end, c).wait_send()
            image_across(image, 0, c).wait_send()
            image_across(image, 1, c).wait_send()
            part(0, c).wait_send()
            row_block(c).wait_send()

    for slot in range(4):
        across(text, slot).wait_send()


def solution(mesh):
    n, m = mesh.shape["inner"], mesh.shape["outer"]

    def per_device(image, text, scale, offset):
        rows, width = image.shape
        dma = pltpu.SemaphoreType.DMA
        block = (rows, width)
        if n == 4:
            body = functools.partial(line4_kernel, m)
            scratch = [
                pltpu.VMEM((4, *block), jnp.bfloat16),
                pltpu.VMEM((4, *block), jnp.bfloat16),
                pltpu.VMEM((4, *block), jnp.bfloat16),
                pltpu.VMEM((2, *block), jnp.float32),
                pltpu.VMEM((2, *block), jnp.bfloat16),
                pltpu.VMEM((2, *block), jnp.bfloat16),
                pltpu.VMEM(block, jnp.bfloat16),
                pltpu.VMEM(block, jnp.bfloat16),
                dma((2,)), dma((4, 2, CHUNKS)), dma((4, CHUNKS)), dma((4,)), dma((4,)),
                dma((CHUNKS,)), dma((CHUNKS,)), dma((2, CHUNKS)), dma((2, CHUNKS)),
                dma((2, CHUNKS)), dma((2, CHUNKS)), dma((CHUNKS,)), dma((CHUNKS,)),
                pltpu.SemaphoreType.REGULAR,
            ]
        else:
            body = functools.partial(kernel, n, m)
            scratch = [
                pltpu.VMEM((2, *block), jnp.bfloat16),
                pltpu.VMEM((2, n, *block), jnp.bfloat16),
                pltpu.VMEM((2, n, *block), jnp.bfloat16),
                dma((2,)), dma((2, n, 2)), dma((2, n)), dma((2, n)), dma((2, n)),
            ]
        return pl.pallas_call(
            body,
            out_shape=(pltpu.VMEM((rows, width), jnp.float32),) * 2,
            in_specs=[pl.BlockSpec(memory_space=pltpu.HBM)] * 2
            + [pl.BlockSpec(memory_space=pltpu.SMEM)] * 2,
            out_specs=(pl.BlockSpec(memory_space=pltpu.VMEM),) * 2,
            scratch_shapes=scratch,
            compiler_params=pltpu.CompilerParams(
                collective_id=0, has_side_effects=True, vmem_limit_bytes=58 * 1024 * 1024
            ),
            cost_estimate=pl.CostEstimate(
                flops=16 * n * rows * rows * width,
                bytes_accessed=12 * rows * width,
                transcendentals=4 * n * rows * rows,
            ),
        )(image, text, scale, offset)

    return jax.shard_map(
        per_device,
        mesh=mesh,
        in_specs=(P(("outer", "inner"), None), P(("outer", "inner"), None), P(), P()),
        out_specs=(P(("outer", "inner"), None), P(("outer", "inner"), None)),
        check_vma=False,
    )
```

```python
import functools

import jax
import jax.numpy as jnp
from jax import lax
from jax.experimental import pallas as pl
from jax.experimental.pallas import tpu as pltpu
from jax.sharding import PartitionSpec as P

MESH = pl.DeviceIdType.MESH
TEXT, IMAGE = 0, 1
CHUNKS = 4
BANDS = 3


def kernel(
    n, m, image, text, scale, offset, grad_image, grad_text,
    own, group, guest, load_sem, line_send, line_recv, side_send, side_recv,
):
    outer, z = lax.axis_index("outer"), lax.axis_index("inner")
    above, below = lax.rem(outer + 1, m), lax.rem(outer + m - 1, m)
    rows = text.shape[0]
    source = (text, image)
    side = (above, below)

    loads = [pltpu.make_async_copy(source[k], own.at[k], load_sem.at[k]) for k in (TEXT, IMAGE)]
    for load in loads:
        load.start()

    barrier = pltpu.get_barrier_semaphore()

    def greet(o, i):
        pl.semaphore_signal(barrier, inc=1, device_id=(o, i), device_id_type=MESH)

    greet(above, z)
    greet(below, z)
    pl.when(z > 0)(lambda: greet(outer, z - 1))
    pl.when(z < n - 1)(lambda: greet(outer, z + 1))
    pl.semaphore_wait(barrier, 2 + (z > 0).astype(jnp.int32) + (z < n - 1).astype(jnp.int32))

    def along(k, src, slot, way):
        return pltpu.make_async_remote_copy(
            src_ref=src,
            dst_ref=group.at[k, slot],
            send_sem=line_send.at[k, slot, way],
            recv_sem=line_recv.at[k, slot],
            device_id=(outer, z + (1 if way else -1)),
            device_id_type=MESH,
        )

    def across(k, src, slot):
        return pltpu.make_async_remote_copy(
            src_ref=src,
            dst_ref=guest.at[k, slot],
            send_sem=side_send.at[k, slot],
            recv_sem=side_recv.at[k, slot],
            device_id=(side[k], z),
            device_id_type=MESH,
        )

    def has_next(way):
        return z < n - 1 if way else z > 0

    def add(k, block, first=False):
        out = (grad_image, grad_text)[k]
        product = lax.dot_general(
            own[1 - k], block[...], (((1,), (1,)), ((), ())), preferred_element_type=jnp.float32
        )
        logit = scale[0] * product + offset[0]
        if first:
            row = lax.broadcasted_iota(jnp.int32, (rows, rows), 0)
            column = lax.broadcasted_iota(jnp.int32, (rows, rows), 1)
            sign = jnp.where(row == column, 1.0, -1.0)
            coef = -sign * jax.nn.sigmoid(-sign * logit) * scale[0]
        else:
            coef = jax.nn.sigmoid(logit) * scale[0]
        term = jnp.dot(coef.astype(jnp.bfloat16), block[...], preferred_element_type=jnp.float32)
        out[...] = term if first else out[...] + term

    for k in (TEXT, IMAGE):
        for way in (1, 0):
            pl.when(has_next(way))(lambda: along(k, source[k], z, way).start())
        across(k, source[k], z).start()

    for load in loads:
        load.wait()
    for k in (TEXT, IMAGE):
        add(k, own.at[k], first=True)

    def visit(k, slot):
        across(k, guest.at[k, slot], slot).wait_recv()
        add(k, guest.at[k, slot])

    visit(TEXT, z)

    def step(s, _):
        def from_line(k):
            for way in (1, 0):
                slot = z - s if way else z + s

                @pl.when(slot >= 0 if way else slot < n)
                def _():
                    along(k, source[k], slot, way).wait_recv()
                    pl.when(has_next(way))(
                        lambda: along(k, group.at[k, slot], slot, way).start()
                    )
                    across(k, group.at[k, slot], slot).start()

            for way in (1, 0):
                slot = z - s if way else z + s
                pl.when(slot >= 0 if way else slot < n)(lambda: add(k, group.at[k, slot]))

        from_line(TEXT)
        pl.when(z - s + 1 >= 0)(lambda: visit(IMAGE, z - s + 1))
        pl.when((z + s - 1 < n) & (s > 1))(lambda: visit(IMAGE, z + s - 1))
        from_line(IMAGE)
        pl.when(z - s >= 0)(lambda: visit(TEXT, z - s))
        pl.when(z + s < n)(lambda: visit(TEXT, z + s))
        return 0

    lax.fori_loop(1, n, step, 0)
    if n > 1:
        pl.when(z - n + 1 >= 0)(lambda: visit(IMAGE, z - n + 1))
        pl.when(z + n - 1 < n)(lambda: visit(IMAGE, z + n - 1))

    def drain(slot, _):
        for k in (TEXT, IMAGE):
            across(k, source[k], slot).wait_send()
            pl.when((slot <= z) & (z < n - 1))(lambda: along(k, source[k], slot, 1).wait_send())
            pl.when((slot >= z) & (z > 0))(lambda: along(k, source[k], slot, 0).wait_send())
        return 0

    lax.fori_loop(0, n, drain, 0)


def line4_kernel(
    m, image, text, scale, offset, grad_image, grad_text,
    group, guest, images, total, part_out, part_in, row_out, row_in,
    load_sem, line_send, line_recv, side_send, side_recv, image_send, image_recv,
    guest_send, guest_recv, part_send, part_recv, row_send, row_recv, turn,
):
    outer, z = lax.axis_index("outer"), lax.axis_index("inner")
    above, below = lax.rem(outer + 1, m), lax.rem(outer + m - 1, m)
    rows, width = text.shape
    size, band = rows // CHUNKS, width // BANDS
    is_end = (z == 0) | (z == 3)
    is_middle = (z == 1) | (z == 2)
    high = (z >= 2).astype(jnp.int32)
    end, middle = 3 * high, 1 + high
    far_end, far_middle = 3 - end, 3 - middle

    loads = [
        pltpu.make_async_copy(image, images.at[0], load_sem.at[0]),
        pltpu.make_async_copy(text, group.at[z], load_sem.at[1]),
    ]
    for load in loads:
        load.start()

    barrier = pltpu.get_barrier_semaphore()

    def greet(o, i):
        pl.semaphore_signal(barrier, inc=1, device_id=(o, i), device_id_type=MESH)

    greet(above, z)
    greet(below, z)
    pl.when(z > 0)(lambda: greet(outer, z - 1))
    pl.when(z < 3)(lambda: greet(outer, z + 1))
    pl.semaphore_wait(barrier, 2 + (z > 0).astype(jnp.int32) + (z < 3).astype(jnp.int32))

    def remote(src, dst, send, recv, o, i):
        return pltpu.make_async_remote_copy(
            src_ref=src, dst_ref=dst, send_sem=send, recv_sem=recv,
            device_id=(o, i), device_id_type=MESH,
        )

    def piece(c):
        return pl.ds(c * size, size)

    def along(src, slot, way, to, c):
        return remote(
            src.at[piece(c)], group.at[slot, piece(c)],
            line_send.at[slot, way, c], line_recv.at[slot, c], outer, to,
        )

    def across(src, slot):
        return remote(src, guest.at[slot], side_send.at[slot], side_recv.at[slot], above, z)

    def image_inward(c):
        return remote(
            image.at[piece(c)], images.at[2, piece(c)],
            image_send.at[c], image_recv.at[c], outer, middle,
        )

    def image_across(src, i, c):
        return remote(
            src.at[piece(c)], images.at[1 + 2 * i, piece(c)],
            guest_send.at[i, c], guest_recv.at[i, c], below, z,
        )

    def columns(c):
        return pl.ds(c * band, band)

    def part(i, c):
        return remote(
            part_out.at[i, :, columns(c)], part_in.at[i, :, columns(c)],
            part_send.at[i, c], part_recv.at[i, c], outer, far_middle,
        )

    def row_block(c):
        return remote(
            row_out.at[:, columns(c)], row_in.at[:, columns(c)],
            row_send.at[c], row_recv.at[c], outer, end,
        )

    def weigh(left, right, match=None):
        product = lax.dot_general(
            left, right, (((1,), (1,)), ((), ())), preferred_element_type=jnp.float32
        )
        logit = scale[0] * product + offset[0]
        if match is not None:
            row = lax.broadcasted_iota(jnp.int32, logit.shape, 0)
            column = lax.broadcasted_iota(jnp.int32, logit.shape, 1)
            sign = jnp.where(column == row + match, 1.0, -1.0)
            coef = -sign * jax.nn.sigmoid(-sign * logit) * scale[0]
        else:
            coef = jax.nn.sigmoid(logit) * scale[0]
        return coef.astype(jnp.bfloat16)

    def pair(left, blocks, match=None):
        right = blocks[...].reshape(-1, width)
        coef = weigh(left, right, match)
        return jnp.dot(coef, right, preferred_element_type=jnp.float32)

    def add_group():
        grad_image[...] = pair(images[0], group, z * rows)

    def add_guest():
        for slot in range(4):
            across(text, slot).wait_recv()
        grad_image[...] += pair(images[0], guest)

    chunks, bands = range(CHUNKS), range(BANDS)

    @pl.when(is_end)
    def _():
        for c in chunks:
            along(text, z, 0, middle, c).start()
        across(text, z).start()
        for c in chunks[:-1]:
            along(text, z, 0, middle, c).wait_send()
        odd = lax.rem(outer, 2) == 1
        pl.when(odd)(lambda: pl.semaphore_wait(turn, 1))
        for c in chunks:
            image_inward(c).start()
        for c in chunks[:-1]:
            image_inward(c).wait_send()
        pl.when(jnp.logical_not(odd) & (outer + 1 < m))(
            lambda: pl.semaphore_signal(
                turn, inc=1, device_id=(above, z), device_id_type=MESH
            )
        )
        for load in loads:
            load.wait()
        for slot in (middle, far_middle, far_end):
            for c in chunks:
                along(text, slot, 0, end, c).wait_recv()
            across(group.at[slot], slot).start()
        add_group()
        add_guest()
        for c in bands:
            row_block(c).wait_recv()
            grad_text[:, columns(c)] = row_in[:, columns(c)].astype(jnp.float32)
        along(text, z, 0, middle, CHUNKS - 1).wait_send()
        image_inward(CHUNKS - 1).wait_send()

    @pl.when(is_middle)
    def _():
        beside, over, far = group.at[end], group.at[far_middle], group.at[far_end]
        for c in chunks:
            along(text, z, 0, far_middle, c).start()
            along(text, z, 1, end, c).start()
        for c in chunks:
            image_across(image, 0, c).start()
        across(text, z).start()
        for load in loads:
            load.wait()
        for c in chunks:
            along(text, end, 0, middle, c).wait_recv()
            along(beside, end, 0, far_middle, c).start()
        across(beside, end).start()
        for c in chunks:
            along(text, far_middle, 0, middle, c).wait_recv()
            along(over, far_middle, 0, end, c).start()
        across(over, far_middle).start()
        first, second = images.at[pl.ds(0, 2)], images.at[pl.ds(2, 2)]
        for c in chunks:
            image_across(image, 0, c).wait_recv()
        total[2] = pair(over[...], first)
        total[1] = pair(beside[...], first)
        for c in chunks:
            if c == CHUNKS // 2:
                total[0] = pair(group[z], first, 0)
            image_inward(c).wait_recv()
            image_across(images.at[2], 1, c).start()
        for c in chunks:
            along(text, far_end, 0, middle, c).wait_recv()
            along(far, far_end, 0, end, c).start()
        for c in chunks:
            image_across(image, 1, c).wait_recv()
        coef = weigh(far[...], images[...].reshape(-1, width))
        for c in bands:
            part_out[1, :, columns(c)] = jnp.dot(
                coef,
                images[:, :, columns(c)].reshape(-1, band),
                preferred_element_type=jnp.float32,
            ).astype(jnp.bfloat16)
            part(1, c).start()
        across(far, far_end).start()
        part_out[0] = (total[2] + pair(over[...], second)).astype(jnp.bfloat16)
        total[1] += pair(beside[...], second, 0)
        for c in bands:
            part(1, c).wait_recv()
            row_out[:, columns(c)] = (
                total[1, :, columns(c)] + part_in[1, :, columns(c)].astype(jnp.float32)
            ).astype(jnp.bfloat16)
            row_block(c).start()
            if c == BANDS - 2:
                for early in bands[:-1]:
                    part(1, early).wait_send()
                for late in bands:
                    part(0, late).start()
        total[0] += pair(group[z], second)
        add_group()
        add_guest()
        for c in bands:
            part(0, c).wait_recv()
            grad_text[:, columns(c)] = (
                total[0, :, columns(c)] + part_in[0, :, columns(c)].astype(jnp.float32)
            )

        part(1, BANDS - 1).wait_send()
        for c in chunks:
            along(text, z, 0, far_middle, c).wait_send()
            along(text, z, 1, end, c).wait_send()
            along(text, end, 0, far_middle, c).wait_send()
            along(text, far_middle, 0, end, c).wait_send()
            along(text, far_end, 0, end, c).wait_send()
            image_across(image, 0, c).wait_send()
            image_across(image, 1, c).wait_send()
        for c in bands:
            part(0, c).wait_send()
            row_block(c).wait_send()

    for slot in range(4):
        across(text, slot).wait_send()


def store_kernel(image_in, text_in, image_out, text_out, sem):
    size = image_in.shape[0] // CHUNKS
    copies = [
        pltpu.make_async_copy(
            src.at[pl.ds(c * size, size)], dst.at[pl.ds(c * size, size)], sem.at[k, c]
        )
        for k, (src, dst) in enumerate(((image_in, image_out), (text_in, text_out)))
        for c in range(CHUNKS)
    ]
    for copy in copies:
        copy.start()
    for copy in copies:
        copy.wait()


def solution(mesh):
    n, m = mesh.shape["inner"], mesh.shape["outer"]

    def per_device(image, text, scale, offset):
        rows, width = image.shape
        dma = pltpu.SemaphoreType.DMA
        block = (rows, width)
        if n == 4:
            body = functools.partial(line4_kernel, m)
            scratch = [
                pltpu.VMEM((4, *block), jnp.bfloat16),
                pltpu.VMEM((4, *block), jnp.bfloat16),
                pltpu.VMEM((4, *block), jnp.bfloat16),
                pltpu.VMEM((3, *block), jnp.float32),
                pltpu.VMEM((2, *block), jnp.bfloat16),
                pltpu.VMEM((2, *block), jnp.bfloat16),
                pltpu.VMEM(block, jnp.bfloat16),
                pltpu.VMEM(block, jnp.bfloat16),
                dma((2,)), dma((4, 2, CHUNKS)), dma((4, CHUNKS)), dma((4,)), dma((4,)),
                dma((CHUNKS,)), dma((CHUNKS,)), dma((2, CHUNKS)), dma((2, CHUNKS)),
                dma((2, BANDS)), dma((2, BANDS)), dma((BANDS,)), dma((BANDS,)),
                pltpu.SemaphoreType.REGULAR,
            ]
        else:
            body = functools.partial(kernel, n, m)
            scratch = [
                pltpu.VMEM((2, *block), jnp.bfloat16),
                pltpu.VMEM((2, n, *block), jnp.bfloat16),
                pltpu.VMEM((2, n, *block), jnp.bfloat16),
                dma((2,)), dma((2, n, 2)), dma((2, n)), dma((2, n)), dma((2, n)),
            ]
        grads = pl.pallas_call(
            body,
            out_shape=(pltpu.VMEM((rows, width), jnp.float32),) * 2,
            in_specs=[pl.BlockSpec(memory_space=pltpu.HBM)] * 2
            + [pl.BlockSpec(memory_space=pltpu.SMEM)] * 2,
            out_specs=(pl.BlockSpec(memory_space=pltpu.VMEM),) * 2,
            scratch_shapes=scratch,
            compiler_params=pltpu.CompilerParams(
                collective_id=0, has_side_effects=True, vmem_limit_bytes=58 * 1024 * 1024
            ),
            cost_estimate=pl.CostEstimate(
                flops=16 * n * rows * rows * width,
                bytes_accessed=12 * rows * width,
                transcendentals=4 * n * rows * rows,
            ),
        )(image, text, scale, offset)
        return pl.pallas_call(
            store_kernel,
            out_shape=(jax.ShapeDtypeStruct(block, jnp.float32),) * 2,
            in_specs=[pl.BlockSpec(memory_space=pl.ANY)] * 2,
            out_specs=(pl.BlockSpec(memory_space=pl.ANY),) * 2,
            scratch_shapes=[dma((2, CHUNKS))],
        )(*grads)

    return jax.shard_map(
        per_device,
        mesh=mesh,
        in_specs=(P(("outer", "inner"), None), P(("outer", "inner"), None), P(), P()),
        out_specs=(P(("outer", "inner"), None), P(("outer", "inner"), None)),
        check_vma=False,
    )
```

```python
import functools

import jax
import jax.numpy as jnp
from jax import lax
from jax.experimental import pallas as pl
from jax.experimental.pallas import tpu as pltpu
from jax.sharding import PartitionSpec as P

MESH = pl.DeviceIdType.MESH
TEXT, IMAGE = 0, 1
CHUNKS = 4


def kernel(
    n, m, image, text, scale, offset, grad_image, grad_text,
    own, group, guest, load_sem, line_send, line_recv, side_send, side_recv,
):
    outer, z = lax.axis_index("outer"), lax.axis_index("inner")
    above, below = lax.rem(outer + 1, m), lax.rem(outer + m - 1, m)
    rows = text.shape[0]
    source = (text, image)
    side = (above, below)

    loads = [pltpu.make_async_copy(source[k], own.at[k], load_sem.at[k]) for k in (TEXT, IMAGE)]
    for load in loads:
        load.start()

    barrier = pltpu.get_barrier_semaphore()

    def greet(o, i):
        pl.semaphore_signal(barrier, inc=1, device_id=(o, i), device_id_type=MESH)

    greet(above, z)
    greet(below, z)
    pl.when(z > 0)(lambda: greet(outer, z - 1))
    pl.when(z < n - 1)(lambda: greet(outer, z + 1))
    pl.semaphore_wait(barrier, 2 + (z > 0).astype(jnp.int32) + (z < n - 1).astype(jnp.int32))

    def along(k, src, slot, way):
        return pltpu.make_async_remote_copy(
            src_ref=src,
            dst_ref=group.at[k, slot],
            send_sem=line_send.at[k, slot, way],
            recv_sem=line_recv.at[k, slot],
            device_id=(outer, z + (1 if way else -1)),
            device_id_type=MESH,
        )

    def across(k, src, slot):
        return pltpu.make_async_remote_copy(
            src_ref=src,
            dst_ref=guest.at[k, slot],
            send_sem=side_send.at[k, slot],
            recv_sem=side_recv.at[k, slot],
            device_id=(side[k], z),
            device_id_type=MESH,
        )

    def has_next(way):
        return z < n - 1 if way else z > 0

    def add(k, block, first=False):
        out = (grad_image, grad_text)[k]
        product = lax.dot_general(
            own[1 - k], block[...], (((1,), (1,)), ((), ())), preferred_element_type=jnp.float32
        )
        logit = scale[0] * product + offset[0]
        if first:
            row = lax.broadcasted_iota(jnp.int32, (rows, rows), 0)
            column = lax.broadcasted_iota(jnp.int32, (rows, rows), 1)
            sign = jnp.where(row == column, 1.0, -1.0)
            coef = -sign * jax.nn.sigmoid(-sign * logit) * scale[0]
        else:
            coef = jax.nn.sigmoid(logit) * scale[0]
        term = jnp.dot(coef.astype(jnp.bfloat16), block[...], preferred_element_type=jnp.float32)
        out[...] = term if first else out[...] + term

    for k in (TEXT, IMAGE):
        for way in (1, 0):
            pl.when(has_next(way))(lambda: along(k, source[k], z, way).start())
        across(k, source[k], z).start()

    for load in loads:
        load.wait()
    for k in (TEXT, IMAGE):
        add(k, own.at[k], first=True)

    def visit(k, slot):
        across(k, guest.at[k, slot], slot).wait_recv()
        add(k, guest.at[k, slot])

    visit(TEXT, z)

    def step(s, _):
        def from_line(k):
            for way in (1, 0):
                slot = z - s if way else z + s

                @pl.when(slot >= 0 if way else slot < n)
                def _():
                    along(k, source[k], slot, way).wait_recv()
                    pl.when(has_next(way))(
                        lambda: along(k, group.at[k, slot], slot, way).start()
                    )
                    across(k, group.at[k, slot], slot).start()

            for way in (1, 0):
                slot = z - s if way else z + s
                pl.when(slot >= 0 if way else slot < n)(lambda: add(k, group.at[k, slot]))

        from_line(TEXT)
        pl.when(z - s + 1 >= 0)(lambda: visit(IMAGE, z - s + 1))
        pl.when((z + s - 1 < n) & (s > 1))(lambda: visit(IMAGE, z + s - 1))
        from_line(IMAGE)
        pl.when(z - s >= 0)(lambda: visit(TEXT, z - s))
        pl.when(z + s < n)(lambda: visit(TEXT, z + s))
        return 0

    lax.fori_loop(1, n, step, 0)
    if n > 1:
        pl.when(z - n + 1 >= 0)(lambda: visit(IMAGE, z - n + 1))
        pl.when(z + n - 1 < n)(lambda: visit(IMAGE, z + n - 1))

    def drain(slot, _):
        for k in (TEXT, IMAGE):
            across(k, source[k], slot).wait_send()
            pl.when((slot <= z) & (z < n - 1))(lambda: along(k, source[k], slot, 1).wait_send())
            pl.when((slot >= z) & (z > 0))(lambda: along(k, source[k], slot, 0).wait_send())
        return 0

    lax.fori_loop(0, n, drain, 0)


def line4_kernel(
    m, image, text, scale, offset, grad_image, grad_text,
    group, guest, images, total, part_out, part_in, row_out, row_in,
    load_sem, line_send, line_recv, side_send, side_recv, image_send, image_recv,
    guest_send, guest_recv, part_send, part_recv, row_send, row_recv,
):
    outer, z = lax.axis_index("outer"), lax.axis_index("inner")
    above, below = lax.rem(outer + 1, m), lax.rem(outer + m - 1, m)
    rows, width = text.shape
    size = rows // CHUNKS
    is_end = (z == 0) | (z == 3)
    is_middle = (z == 1) | (z == 2)
    high = (z >= 2).astype(jnp.int32)
    end, middle = 3 * high, 1 + high
    far_end, far_middle = 3 - end, 3 - middle

    loads = [
        pltpu.make_async_copy(image, images.at[0], load_sem.at[0]),
        pltpu.make_async_copy(text, group.at[z], load_sem.at[1]),
    ]
    for load in loads:
        load.start()

    barrier = pltpu.get_barrier_semaphore()

    def greet(o, i):
        pl.semaphore_signal(barrier, inc=1, device_id=(o, i), device_id_type=MESH)

    greet(above, z)
    greet(below, z)
    pl.when(z > 0)(lambda: greet(outer, z - 1))
    pl.when(z < 3)(lambda: greet(outer, z + 1))
    pl.semaphore_wait(barrier, 2 + (z > 0).astype(jnp.int32) + (z < 3).astype(jnp.int32))

    def remote(src, dst, send, recv, o, i):
        return pltpu.make_async_remote_copy(
            src_ref=src, dst_ref=dst, send_sem=send, recv_sem=recv,
            device_id=(o, i), device_id_type=MESH,
        )

    def piece(c):
        return pl.ds(c * size, size)

    def along(src, slot, way, to, c):
        return remote(
            src.at[piece(c)], group.at[slot, piece(c)],
            line_send.at[slot, way, c], line_recv.at[slot, c], outer, to,
        )

    def across(src, slot):
        return remote(src, guest.at[slot], side_send.at[slot], side_recv.at[slot], above, z)

    def image_inward(c):
        return remote(
            image.at[piece(c)], images.at[2, piece(c)],
            image_send.at[c], image_recv.at[c], outer, middle,
        )

    def image_across(src, i, c):
        return remote(
            src.at[piece(c)], images.at[1 + 2 * i, piece(c)],
            guest_send.at[i, c], guest_recv.at[i, c], below, z,
        )

    def part(i, c):
        return remote(
            part_out.at[i, piece(c)], part_in.at[i, piece(c)],
            part_send.at[i, c], part_recv.at[i, c], outer, far_middle,
        )

    def row_block(c):
        return remote(
            row_out.at[piece(c)], row_in.at[piece(c)], row_send.at[c], row_recv.at[c], outer, end
        )

    def weigh(left, right, match=None):
        product = lax.dot_general(
            left, right, (((1,), (1,)), ((), ())), preferred_element_type=jnp.float32
        )
        logit = scale[0] * product + offset[0]
        if match is not None:
            row = lax.broadcasted_iota(jnp.int32, logit.shape, 0)
            column = lax.broadcasted_iota(jnp.int32, logit.shape, 1)
            sign = jnp.where(column == row + match, 1.0, -1.0)
            coef = -sign * jax.nn.sigmoid(-sign * logit) * scale[0]
        else:
            coef = jax.nn.sigmoid(logit) * scale[0]
        return coef.astype(jnp.bfloat16)

    def pair(left, blocks, match=None):
        right = blocks[...].reshape(-1, width)
        coef = weigh(left, right, match)
        return jnp.dot(coef, right, preferred_element_type=jnp.float32)

    def add_group():
        grad_image[...] = pair(images[0], group, z * rows)

    def add_guest():
        for slot in range(4):
            across(text, slot).wait_recv()
        grad_image[...] += pair(images[0], guest)

    chunks = range(CHUNKS)

    @pl.when(is_end)
    def _():
        for c in chunks:
            image_inward(c).start()
        across(text, z).start()
        for load in loads:
            load.wait()
        for c in chunks[:-1]:
            image_inward(c).wait_send()
        for c in chunks:
            along(text, z, 0, middle, c).start()
        for slot in (middle, far_middle, far_end):
            for c in chunks:
                along(text, slot, 0, end, c).wait_recv()
            across(group.at[slot], slot).start()
        add_group()
        add_guest()
        for c in chunks:
            row_block(c).wait_recv()
            grad_text[piece(c), :] = row_in[piece(c), :].astype(jnp.float32)
        image_inward(CHUNKS - 1).wait_send()
        for c in chunks:
            along(text, z, 0, middle, c).wait_send()

    @pl.when(is_middle)
    def _():
        beside, over, far = group.at[end], group.at[far_middle], group.at[far_end]
        first, second = images.at[pl.ds(0, 2)], images.at[pl.ds(2, 2)]
        for c in chunks:
            along(text, z, 0, far_middle, c).start()
            along(text, z, 1, end, c).start()
        for c in chunks:
            image_across(image, 0, c).start()
        across(text, z).start()
        for load in loads:
            load.wait()
        for c in chunks:
            image_inward(c).wait_recv()
            image_across(images.at[2], 1, c).start()
            along(text, far_middle, 0, middle, c).wait_recv()
            along(over, far_middle, 0, end, c).start()
        across(over, far_middle).start()
        for c in chunks:
            image_across(image, 0, c).wait_recv()
        total[2] = pair(over[...], first)
        total[0] = pair(group[z], first, 0)
        for c in chunks:
            along(text, end, 0, middle, c).wait_recv()
            along(beside, end, 0, far_middle, c).start()
        for c in chunks:
            image_across(image, 1, c).wait_recv()
        part_out[0] = (total[2] + pair(over[...], second)).astype(jnp.bfloat16)
        for c in chunks[: CHUNKS // 2]:
            part(0, c).start()
        across(beside, end).start()
        for c in chunks:
            along(text, far_end, 0, middle, c).wait_recv()
            along(far, far_end, 0, end, c).start()
        part_out[1] = pair(far[...], images).astype(jnp.bfloat16)
        for c in chunks:
            part(1, c).start()
        across(far, far_end).start()
        total[1] = pair(beside[...], images, 2 * rows)
        for c in chunks:
            part(1, c).wait_recv()
            row_out[piece(c), :] = (
                total[1, piece(c), :] + part_in[1, piece(c), :].astype(jnp.float32)
            ).astype(jnp.bfloat16)
            row_block(c).start()
            if c == CHUNKS - 2:
                for early in chunks[:-1]:
                    part(1, early).wait_send()
                for late in chunks[CHUNKS // 2 :]:
                    part(0, late).start()
        total[0] += pair(group[z], second)
        add_group()
        add_guest()
        for c in chunks:
            part(0, c).wait_recv()
            grad_text[piece(c), :] = (
                total[0, piece(c), :] + part_in[0, piece(c), :].astype(jnp.float32)
            )

        part(1, CHUNKS - 1).wait_send()
        for c in chunks:
            along(text, z, 0, far_middle, c).wait_send()
            along(text, z, 1, end, c).wait_send()
            along(text, end, 0, far_middle, c).wait_send()
            along(text, far_middle, 0, end, c).wait_send()
            along(text, far_end, 0, end, c).wait_send()
            image_across(image, 0, c).wait_send()
            image_across(image, 1, c).wait_send()
            part(0, c).wait_send()
            row_block(c).wait_send()

    for slot in range(4):
        across(text, slot).wait_send()


def solution(mesh):
    n, m = mesh.shape["inner"], mesh.shape["outer"]

    def per_device(image, text, scale, offset):
        rows, width = image.shape
        dma = pltpu.SemaphoreType.DMA
        block = (rows, width)
        if n == 4:
            body = functools.partial(line4_kernel, m)
            scratch = [
                pltpu.VMEM((4, *block), jnp.bfloat16),
                pltpu.VMEM((4, *block), jnp.bfloat16),
                pltpu.VMEM((4, *block), jnp.bfloat16),
                pltpu.VMEM((3, *block), jnp.float32),
                pltpu.VMEM((2, *block), jnp.bfloat16),
                pltpu.VMEM((2, *block), jnp.bfloat16),
                pltpu.VMEM(block, jnp.bfloat16),
                pltpu.VMEM(block, jnp.bfloat16),
                dma((2,)), dma((4, 2, CHUNKS)), dma((4, CHUNKS)), dma((4,)), dma((4,)),
                dma((CHUNKS,)), dma((CHUNKS,)), dma((2, CHUNKS)), dma((2, CHUNKS)),
                dma((2, CHUNKS)), dma((2, CHUNKS)), dma((CHUNKS,)), dma((CHUNKS,)),
            ]
        else:
            body = functools.partial(kernel, n, m)
            scratch = [
                pltpu.VMEM((2, *block), jnp.bfloat16),
                pltpu.VMEM((2, n, *block), jnp.bfloat16),
                pltpu.VMEM((2, n, *block), jnp.bfloat16),
                dma((2,)), dma((2, n, 2)), dma((2, n)), dma((2, n)), dma((2, n)),
            ]
        return pl.pallas_call(
            body,
            out_shape=(pltpu.VMEM((rows, width), jnp.float32),) * 2,
            in_specs=[pl.BlockSpec(memory_space=pltpu.HBM)] * 2
            + [pl.BlockSpec(memory_space=pltpu.SMEM)] * 2,
            out_specs=(pl.BlockSpec(memory_space=pltpu.VMEM),) * 2,
            scratch_shapes=scratch,
            compiler_params=pltpu.CompilerParams(
                collective_id=0, has_side_effects=True, vmem_limit_bytes=58 * 1024 * 1024
            ),
            cost_estimate=pl.CostEstimate(
                flops=16 * n * rows * rows * width,
                bytes_accessed=12 * rows * width,
                transcendentals=4 * n * rows * rows,
            ),
        )(image, text, scale, offset)

    return jax.shard_map(
        per_device,
        mesh=mesh,
        in_specs=(P(("outer", "inner"), None), P(("outer", "inner"), None), P(), P()),
        out_specs=(P(("outer", "inner"), None), P(("outer", "inner"), None)),
        check_vma=False,
    )
```

```python
import functools

import jax
import jax.numpy as jnp
from jax import lax
from jax.experimental import pallas as pl
from jax.experimental.pallas import tpu as pltpu
from jax.sharding import PartitionSpec as P

MESH = pl.DeviceIdType.MESH
TEXT, IMAGE = 0, 1
CHUNKS = 4


def kernel(
    n, m, image, text, scale, offset, grad_image, grad_text,
    own, group, guest, load_sem, line_send, line_recv, side_send, side_recv,
):
    outer, z = lax.axis_index("outer"), lax.axis_index("inner")
    above, below = lax.rem(outer + 1, m), lax.rem(outer + m - 1, m)
    rows = text.shape[0]
    source = (text, image)
    side = (above, below)

    loads = [pltpu.make_async_copy(source[k], own.at[k], load_sem.at[k]) for k in (TEXT, IMAGE)]
    for load in loads:
        load.start()

    barrier = pltpu.get_barrier_semaphore()

    def greet(o, i):
        pl.semaphore_signal(barrier, inc=1, device_id=(o, i), device_id_type=MESH)

    greet(above, z)
    greet(below, z)
    pl.when(z > 0)(lambda: greet(outer, z - 1))
    pl.when(z < n - 1)(lambda: greet(outer, z + 1))
    pl.semaphore_wait(barrier, 2 + (z > 0).astype(jnp.int32) + (z < n - 1).astype(jnp.int32))

    def along(k, src, slot, way):
        return pltpu.make_async_remote_copy(
            src_ref=src,
            dst_ref=group.at[k, slot],
            send_sem=line_send.at[k, slot, way],
            recv_sem=line_recv.at[k, slot],
            device_id=(outer, z + (1 if way else -1)),
            device_id_type=MESH,
        )

    def across(k, src, slot):
        return pltpu.make_async_remote_copy(
            src_ref=src,
            dst_ref=guest.at[k, slot],
            send_sem=side_send.at[k, slot],
            recv_sem=side_recv.at[k, slot],
            device_id=(side[k], z),
            device_id_type=MESH,
        )

    def has_next(way):
        return z < n - 1 if way else z > 0

    def add(k, block, first=False):
        out = (grad_image, grad_text)[k]
        product = lax.dot_general(
            own[1 - k], block[...], (((1,), (1,)), ((), ())), preferred_element_type=jnp.float32
        )
        logit = scale[0] * product + offset[0]
        if first:
            row = lax.broadcasted_iota(jnp.int32, (rows, rows), 0)
            column = lax.broadcasted_iota(jnp.int32, (rows, rows), 1)
            sign = jnp.where(row == column, 1.0, -1.0)
            coef = -sign * jax.nn.sigmoid(-sign * logit) * scale[0]
        else:
            coef = jax.nn.sigmoid(logit) * scale[0]
        term = jnp.dot(coef.astype(jnp.bfloat16), block[...], preferred_element_type=jnp.float32)
        out[...] = term if first else out[...] + term

    for k in (TEXT, IMAGE):
        for way in (1, 0):
            pl.when(has_next(way))(lambda: along(k, source[k], z, way).start())
        across(k, source[k], z).start()

    for load in loads:
        load.wait()
    for k in (TEXT, IMAGE):
        add(k, own.at[k], first=True)

    def visit(k, slot):
        across(k, guest.at[k, slot], slot).wait_recv()
        add(k, guest.at[k, slot])

    visit(TEXT, z)

    def step(s, _):
        def from_line(k):
            for way in (1, 0):
                slot = z - s if way else z + s

                @pl.when(slot >= 0 if way else slot < n)
                def _():
                    along(k, source[k], slot, way).wait_recv()
                    pl.when(has_next(way))(
                        lambda: along(k, group.at[k, slot], slot, way).start()
                    )
                    across(k, group.at[k, slot], slot).start()

            for way in (1, 0):
                slot = z - s if way else z + s
                pl.when(slot >= 0 if way else slot < n)(lambda: add(k, group.at[k, slot]))

        from_line(TEXT)
        pl.when(z - s + 1 >= 0)(lambda: visit(IMAGE, z - s + 1))
        pl.when((z + s - 1 < n) & (s > 1))(lambda: visit(IMAGE, z + s - 1))
        from_line(IMAGE)
        pl.when(z - s >= 0)(lambda: visit(TEXT, z - s))
        pl.when(z + s < n)(lambda: visit(TEXT, z + s))
        return 0

    lax.fori_loop(1, n, step, 0)
    if n > 1:
        pl.when(z - n + 1 >= 0)(lambda: visit(IMAGE, z - n + 1))
        pl.when(z + n - 1 < n)(lambda: visit(IMAGE, z + n - 1))

    def drain(slot, _):
        for k in (TEXT, IMAGE):
            across(k, source[k], slot).wait_send()
            pl.when((slot <= z) & (z < n - 1))(lambda: along(k, source[k], slot, 1).wait_send())
            pl.when((slot >= z) & (z > 0))(lambda: along(k, source[k], slot, 0).wait_send())
        return 0

    lax.fori_loop(0, n, drain, 0)


def line4_kernel(
    m, image, text, scale, offset, grad_image, grad_text,
    group, guest, images, total, part_out, part_in, row_out, row_in,
    load_sem, line_send, line_recv, side_send, side_recv, image_send, image_recv,
    guest_send, guest_recv, part_send, part_recv, row_send, row_recv,
):
    outer, z = lax.axis_index("outer"), lax.axis_index("inner")
    above, below = lax.rem(outer + 1, m), lax.rem(outer + m - 1, m)
    rows, width = text.shape
    size = rows // CHUNKS
    is_end = (z == 0) | (z == 3)
    is_middle = (z == 1) | (z == 2)
    high = (z >= 2).astype(jnp.int32)
    end, middle = 3 * high, 1 + high
    far_end, far_middle = 3 - end, 3 - middle

    loads = [
        pltpu.make_async_copy(image, images.at[0], load_sem.at[0]),
        pltpu.make_async_copy(text, group.at[z], load_sem.at[1]),
    ]
    for load in loads:
        load.start()

    barrier = pltpu.get_barrier_semaphore()

    def greet(o, i):
        pl.semaphore_signal(barrier, inc=1, device_id=(o, i), device_id_type=MESH)

    greet(above, z)
    greet(below, z)
    pl.when(z > 0)(lambda: greet(outer, z - 1))
    pl.when(z < 3)(lambda: greet(outer, z + 1))
    pl.semaphore_wait(barrier, 2 + (z > 0).astype(jnp.int32) + (z < 3).astype(jnp.int32))

    def remote(src, dst, send, recv, o, i):
        return pltpu.make_async_remote_copy(
            src_ref=src, dst_ref=dst, send_sem=send, recv_sem=recv,
            device_id=(o, i), device_id_type=MESH,
        )

    def piece(c):
        return pl.ds(c * size, size)

    def along(src, slot, way, to, c):
        return remote(
            src.at[piece(c)], group.at[slot, piece(c)],
            line_send.at[slot, way, c], line_recv.at[slot, c], outer, to,
        )

    def across(src, slot, c):
        return remote(
            src.at[piece(c)], guest.at[slot, piece(c)],
            side_send.at[slot, c], side_recv.at[slot, c], above, z,
        )

    def image_inward(c):
        return remote(
            image.at[piece(c)], images.at[2, piece(c)],
            image_send.at[c], image_recv.at[c], outer, middle,
        )

    def image_across(src, i, c):
        return remote(
            src.at[piece(c)], images.at[1 + 2 * i, piece(c)],
            guest_send.at[i, c], guest_recv.at[i, c], below, z,
        )

    def part(i, c):
        return remote(
            part_out.at[i, piece(c)], part_in.at[i, piece(c)],
            part_send.at[i, c], part_recv.at[i, c], outer, far_middle,
        )

    def row_block(c):
        return remote(
            row_out.at[piece(c)], row_in.at[piece(c)], row_send.at[c], row_recv.at[c], outer, end
        )

    def weigh(left, right, match=None):
        product = lax.dot_general(
            left, right, (((1,), (1,)), ((), ())), preferred_element_type=jnp.float32
        )
        logit = scale[0] * product + offset[0]
        if match is not None:
            row = lax.broadcasted_iota(jnp.int32, logit.shape, 0)
            column = lax.broadcasted_iota(jnp.int32, logit.shape, 1)
            sign = jnp.where(column == row + match, 1.0, -1.0)
            coef = -sign * jax.nn.sigmoid(-sign * logit) * scale[0]
        else:
            coef = jax.nn.sigmoid(logit) * scale[0]
        return coef.astype(jnp.bfloat16)

    def pair(left, blocks, match=None):
        right = blocks[...].reshape(-1, width)
        coef = weigh(left, right, match)
        return jnp.dot(coef, right, preferred_element_type=jnp.float32)

    def add_group(slot, count, match=None, first=False):
        term = pair(images[0], group.at[pl.ds(slot, count)], match)
        grad_image[...] = term if first else grad_image[...] + term

    def add_guest(slot, count):
        for k in range(count):
            for c in chunks:
                across(text, slot + k, c).wait_recv()
        grad_image[...] += pair(images[0], guest.at[pl.ds(slot, count)])

    chunks = range(CHUNKS)

    @pl.when(is_end)
    def _():
        for c in chunks:
            image_inward(c).start()
        for c in chunks:
            across(text, z, c).start()
        for load in loads:
            load.wait()
        for c in chunks[:-1]:
            image_inward(c).wait_send()
        for c in chunks:
            along(text, z, 0, middle, c).start()
        add_group(z, 1, 0, first=True)
        for slot in (middle, far_middle, far_end):
            for c in chunks:
                along(text, slot, 0, end, c).wait_recv()
                across(group.at[slot], slot, c).start()
        add_group(1, 2)
        add_group(far_end, 1)
        add_guest(end, 1)
        add_guest(1, 2)
        add_guest(far_end, 1)
        for c in chunks:
            row_block(c).wait_recv()
            grad_text[piece(c), :] = row_in[piece(c), :].astype(jnp.float32)
        image_inward(CHUNKS - 1).wait_send()
        for c in chunks:
            along(text, z, 0, middle, c).wait_send()

    @pl.when(is_middle)
    def _():
        beside, over, far = group.at[end], group.at[far_middle], group.at[far_end]
        first, second = images.at[pl.ds(0, 2)], images.at[pl.ds(2, 2)]
        for c in chunks:
            along(text, z, 0, far_middle, c).start()
            along(text, z, 1, end, c).start()
        for c in chunks:
            image_across(image, 0, c).start()
        for c in chunks:
            across(text, z, c).start()
        for load in loads:
            load.wait()
        for c in chunks:
            image_inward(c).wait_recv()
            image_across(images.at[2], 1, c).start()
            along(text, far_middle, 0, middle, c).wait_recv()
            along(over, far_middle, 0, end, c).start()
            across(over, far_middle, c).start()
        for c in chunks:
            image_across(image, 0, c).wait_recv()
        total[2] = pair(over[...], first)
        for c in chunks:
            along(text, end, 0, middle, c).wait_recv()
            along(beside, end, 0, far_middle, c).start()
            across(beside, end, c).start()
            if c == 0:
                total[0] = pair(group[z], first, 0)
            if c == 1:
                add_group(1, 2, (z - 1) * rows, first=True)
        for c in chunks:
            image_across(image, 1, c).wait_recv()
        part_out[0] = (total[2] + pair(over[...], second)).astype(jnp.bfloat16)
        for c in chunks[: CHUNKS // 2]:
            part(0, c).start()
        for c in chunks:
            along(text, far_end, 0, middle, c).wait_recv()
            along(far, far_end, 0, end, c).start()
            across(far, far_end, c).start()
        part_out[1] = pair(far[...], images).astype(jnp.bfloat16)
        for c in chunks:
            part(1, c).start()
        total[1] = pair(beside[...], images, 2 * rows)
        total[0] += pair(group[z], second)
        between = (
            lambda: add_group(end, 1),
            lambda: add_group(far_end, 1),
            lambda: add_guest(1, 2),
            lambda: add_guest(end, 1),
        )
        gate = CHUNKS // 2 - 1
        for c in chunks:
            part(1, c).wait_recv()
            row_out[piece(c), :] = (
                total[1, piece(c), :] + part_in[1, piece(c), :].astype(jnp.float32)
            ).astype(jnp.bfloat16)
            row_block(c).start()
            if c == gate:
                for early in chunks[: gate + 1]:
                    part(1, early).wait_send()
                for late in chunks[CHUNKS // 2 :]:
                    part(0, late).start()
            if c < len(between):
                between[c]()
        add_guest(far_end, 1)
        for c in chunks:
            part(0, c).wait_recv()
            grad_text[piece(c), :] = (
                total[0, piece(c), :] + part_in[0, piece(c), :].astype(jnp.float32)
            )

        for c in chunks[gate + 1 :]:
            part(1, c).wait_send()
        for c in chunks:
            along(text, z, 0, far_middle, c).wait_send()
            along(text, z, 1, end, c).wait_send()
            along(text, end, 0, far_middle, c).wait_send()
            along(text, far_middle, 0, end, c).wait_send()
            along(text, far_end, 0, end, c).wait_send()
            image_across(image, 0, c).wait_send()
            image_across(image, 1, c).wait_send()
            part(0, c).wait_send()
            row_block(c).wait_send()

    for slot in range(4):
        for c in chunks:
            across(text, slot, c).wait_send()


def solution(mesh):
    n, m = mesh.shape["inner"], mesh.shape["outer"]

    def per_device(image, text, scale, offset):
        rows, width = image.shape
        dma = pltpu.SemaphoreType.DMA
        block = (rows, width)
        if n == 4:
            body = functools.partial(line4_kernel, m)
            scratch = [
                pltpu.VMEM((4, *block), jnp.bfloat16),
                pltpu.VMEM((4, *block), jnp.bfloat16),
                pltpu.VMEM((4, *block), jnp.bfloat16),
                pltpu.VMEM((3, *block), jnp.float32),
                pltpu.VMEM((2, *block), jnp.bfloat16),
                pltpu.VMEM((2, *block), jnp.bfloat16),
                pltpu.VMEM(block, jnp.bfloat16),
                pltpu.VMEM(block, jnp.bfloat16),
                dma((2,)), dma((4, 2, CHUNKS)), dma((4, CHUNKS)), dma((4, CHUNKS)), dma((4, CHUNKS)),
                dma((CHUNKS,)), dma((CHUNKS,)), dma((2, CHUNKS)), dma((2, CHUNKS)),
                dma((2, CHUNKS)), dma((2, CHUNKS)), dma((CHUNKS,)), dma((CHUNKS,)),
            ]
        else:
            body = functools.partial(kernel, n, m)
            scratch = [
                pltpu.VMEM((2, *block), jnp.bfloat16),
                pltpu.VMEM((2, n, *block), jnp.bfloat16),
                pltpu.VMEM((2, n, *block), jnp.bfloat16),
                dma((2,)), dma((2, n, 2)), dma((2, n)), dma((2, n)), dma((2, n)),
            ]
        return pl.pallas_call(
            body,
            out_shape=(pltpu.VMEM((rows, width), jnp.float32),) * 2,
            in_specs=[pl.BlockSpec(memory_space=pltpu.HBM)] * 2
            + [pl.BlockSpec(memory_space=pltpu.SMEM)] * 2,
            out_specs=(pl.BlockSpec(memory_space=pltpu.VMEM),) * 2,
            scratch_shapes=scratch,
            compiler_params=pltpu.CompilerParams(
                collective_id=0, has_side_effects=True, vmem_limit_bytes=58 * 1024 * 1024
            ),
            cost_estimate=pl.CostEstimate(
                flops=16 * n * rows * rows * width,
                bytes_accessed=12 * rows * width,
                transcendentals=4 * n * rows * rows,
            ),
        )(image, text, scale, offset)

    return jax.shard_map(
        per_device,
        mesh=mesh,
        in_specs=(P(("outer", "inner"), None), P(("outer", "inner"), None), P(), P()),
        out_specs=(P(("outer", "inner"), None), P(("outer", "inner"), None)),
        check_vma=False,
    )
```

```python
import functools

import jax
import jax.numpy as jnp
from jax import lax
from jax.experimental import pallas as pl
from jax.experimental.pallas import tpu as pltpu
from jax.sharding import PartitionSpec as P

MESH = pl.DeviceIdType.MESH
TEXT, IMAGE = 0, 1
CHUNKS = 8
AHEAD = 3


def kernel(
    n, m, image, text, scale, offset, grad_image, grad_text,
    own, group, guest, load_sem, line_send, line_recv, side_send, side_recv,
):
    outer, z = lax.axis_index("outer"), lax.axis_index("inner")
    above, below = lax.rem(outer + 1, m), lax.rem(outer + m - 1, m)
    rows = text.shape[0]
    source = (text, image)
    side = (above, below)

    loads = [pltpu.make_async_copy(source[k], own.at[k], load_sem.at[k]) for k in (TEXT, IMAGE)]
    for load in loads:
        load.start()

    barrier = pltpu.get_barrier_semaphore()

    def greet(o, i):
        pl.semaphore_signal(barrier, inc=1, device_id=(o, i), device_id_type=MESH)

    greet(above, z)
    greet(below, z)
    pl.when(z > 0)(lambda: greet(outer, z - 1))
    pl.when(z < n - 1)(lambda: greet(outer, z + 1))
    pl.semaphore_wait(barrier, 2 + (z > 0).astype(jnp.int32) + (z < n - 1).astype(jnp.int32))

    def along(k, src, slot, way):
        return pltpu.make_async_remote_copy(
            src_ref=src,
            dst_ref=group.at[k, slot],
            send_sem=line_send.at[k, slot, way],
            recv_sem=line_recv.at[k, slot],
            device_id=(outer, z + (1 if way else -1)),
            device_id_type=MESH,
        )

    def across(k, src, slot):
        return pltpu.make_async_remote_copy(
            src_ref=src,
            dst_ref=guest.at[k, slot],
            send_sem=side_send.at[k, slot],
            recv_sem=side_recv.at[k, slot],
            device_id=(side[k], z),
            device_id_type=MESH,
        )

    def has_next(way):
        return z < n - 1 if way else z > 0

    def add(k, block, first=False):
        out = (grad_image, grad_text)[k]
        product = lax.dot_general(
            own[1 - k], block[...], (((1,), (1,)), ((), ())), preferred_element_type=jnp.float32
        )
        logit = scale[0] * product + offset[0]
        if first:
            row = lax.broadcasted_iota(jnp.int32, (rows, rows), 0)
            column = lax.broadcasted_iota(jnp.int32, (rows, rows), 1)
            sign = jnp.where(row == column, 1.0, -1.0)
            coef = -sign * jax.nn.sigmoid(-sign * logit) * scale[0]
        else:
            coef = jax.nn.sigmoid(logit) * scale[0]
        term = jnp.dot(coef.astype(jnp.bfloat16), block[...], preferred_element_type=jnp.float32)
        out[...] = term if first else out[...] + term

    for k in (TEXT, IMAGE):
        for way in (1, 0):
            pl.when(has_next(way))(lambda: along(k, source[k], z, way).start())
        across(k, source[k], z).start()

    for load in loads:
        load.wait()
    for k in (TEXT, IMAGE):
        add(k, own.at[k], first=True)

    def visit(k, slot):
        across(k, guest.at[k, slot], slot).wait_recv()
        add(k, guest.at[k, slot])

    visit(TEXT, z)

    def step(s, _):
        def from_line(k):
            for way in (1, 0):
                slot = z - s if way else z + s

                @pl.when(slot >= 0 if way else slot < n)
                def _():
                    along(k, source[k], slot, way).wait_recv()
                    pl.when(has_next(way))(
                        lambda: along(k, group.at[k, slot], slot, way).start()
                    )
                    across(k, group.at[k, slot], slot).start()

            for way in (1, 0):
                slot = z - s if way else z + s
                pl.when(slot >= 0 if way else slot < n)(lambda: add(k, group.at[k, slot]))

        from_line(TEXT)
        pl.when(z - s + 1 >= 0)(lambda: visit(IMAGE, z - s + 1))
        pl.when((z + s - 1 < n) & (s > 1))(lambda: visit(IMAGE, z + s - 1))
        from_line(IMAGE)
        pl.when(z - s >= 0)(lambda: visit(TEXT, z - s))
        pl.when(z + s < n)(lambda: visit(TEXT, z + s))
        return 0

    lax.fori_loop(1, n, step, 0)
    if n > 1:
        pl.when(z - n + 1 >= 0)(lambda: visit(IMAGE, z - n + 1))
        pl.when(z + n - 1 < n)(lambda: visit(IMAGE, z + n - 1))

    def drain(slot, _):
        for k in (TEXT, IMAGE):
            across(k, source[k], slot).wait_send()
            pl.when((slot <= z) & (z < n - 1))(lambda: along(k, source[k], slot, 1).wait_send())
            pl.when((slot >= z) & (z > 0))(lambda: along(k, source[k], slot, 0).wait_send())
        return 0

    lax.fori_loop(0, n, drain, 0)


def line4_kernel(
    m, image, text, scale_in, offset_in, grad_image, grad_text, scale, offset,
    group, guest, images, total, part_out, part_in, row_out, row_in,
    load_sem, line_send, line_recv, side_send, side_recv, image_send, image_recv,
    guest_send, guest_recv, part_send, part_recv, row_send, row_recv,
):
    outer, z = lax.axis_index("outer"), lax.axis_index("inner")
    above, below = lax.rem(outer + 1, m), lax.rem(outer + m - 1, m)
    rows, width = text.shape
    size = rows // CHUNKS
    is_end = (z == 0) | (z == 3)
    is_middle = (z == 1) | (z == 2)
    high = (z >= 2).astype(jnp.int32)
    end, middle = 3 * high, 1 + high
    far_end, far_middle = 3 - end, 3 - middle

    loads = [
        pltpu.make_async_copy(image, images.at[0], load_sem.at[0]),
        pltpu.make_async_copy(text, group.at[z], load_sem.at[1]),
        pltpu.make_async_copy(scale_in, scale, load_sem.at[2]),
        pltpu.make_async_copy(offset_in, offset, load_sem.at[3]),
    ]
    for load in loads:
        load.start()

    barrier = pltpu.get_barrier_semaphore()

    def greet(o, i):
        pl.semaphore_signal(barrier, inc=1, device_id=(o, i), device_id_type=MESH)

    greet(above, z)
    greet(below, z)
    pl.when(z > 0)(lambda: greet(outer, z - 1))
    pl.when(z < 3)(lambda: greet(outer, z + 1))
    pl.semaphore_wait(barrier, 2 + (z > 0).astype(jnp.int32) + (z < 3).astype(jnp.int32))

    def remote(src, dst, send, recv, o, i):
        return pltpu.make_async_remote_copy(
            src_ref=src, dst_ref=dst, send_sem=send, recv_sem=recv,
            device_id=(o, i), device_id_type=MESH,
        )

    def piece(c):
        return pl.ds(c * size, size)

    def along(src, slot, way, to, c):
        return remote(
            src.at[piece(c)], group.at[slot, piece(c)],
            line_send.at[slot, way, c], line_recv.at[slot, c], outer, to,
        )

    def across(src, slot, c):
        return remote(
            src.at[piece(c)], guest.at[slot, piece(c)],
            side_send.at[slot, c], side_recv.at[slot, c], above, z,
        )

    def image_inward(c):
        return remote(
            image.at[piece(c)], images.at[2, piece(c)],
            image_send.at[c], image_recv.at[c], outer, middle,
        )

    def image_across(src, i, c):
        return remote(
            src.at[piece(c)], images.at[1 + 2 * i, piece(c)],
            guest_send.at[i, c], guest_recv.at[i, c], below, z,
        )

    def part(i, c):
        return remote(
            part_out.at[i, piece(c)], part_in.at[i, piece(c)],
            part_send.at[i, c], part_recv.at[i, c], outer, far_middle,
        )

    def row_block(c):
        return remote(
            row_out.at[piece(c)], row_in.at[piece(c)], row_send.at[c], row_recv.at[c], outer, end
        )

    def weigh(left, right, match=None):
        product = lax.dot_general(
            left, right, (((1,), (1,)), ((), ())), preferred_element_type=jnp.float32
        )
        logit = scale[0] * product + offset[0]
        if match is not None:
            row = lax.broadcasted_iota(jnp.int32, logit.shape, 0)
            column = lax.broadcasted_iota(jnp.int32, logit.shape, 1)
            sign = jnp.where(column == row + match, 1.0, -1.0)
            coef = -sign * jax.nn.sigmoid(-sign * logit) * scale[0]
        else:
            coef = jax.nn.sigmoid(logit) * scale[0]
        return coef.astype(jnp.bfloat16)

    def pair(left, blocks, match=None):
        right = blocks[...].reshape(-1, width)
        coef = weigh(left, right, match)
        return jnp.dot(coef, right, preferred_element_type=jnp.float32)

    def add_group(slot, count, match=None, first=False):
        term = pair(images[0], group.at[pl.ds(slot, count)], match)
        grad_image[...] = term if first else grad_image[...] + term

    def add_guest(slot, count):
        for k in range(count):
            for c in chunks:
                across(text, slot + k, c).wait_recv()
        grad_image[...] += pair(images[0], guest.at[pl.ds(slot, count)])

    chunks = range(CHUNKS)

    @pl.when(is_end)
    def _():
        for c in chunks:
            image_inward(c).start()
        for c in chunks:
            across(text, z, c).start()
        for load in loads:
            load.wait()
        for c in chunks[:-1]:
            image_inward(c).wait_send()
        for c in chunks:
            along(text, z, 0, middle, c).start()
        add_group(z, 1, 0, first=True)
        for slot in (middle, far_middle, far_end):
            for c in chunks:
                along(text, slot, 0, end, c).wait_recv()
                across(group.at[slot], slot, c).start()
        add_group(1, 2)
        add_group(far_end, 1)
        add_guest(end, 1)
        add_guest(1, 2)
        add_guest(far_end, 1)
        for c in chunks:
            row_block(c).wait_recv()
            grad_text[piece(c), :] = row_in[piece(c), :].astype(jnp.float32)
        image_inward(CHUNKS - 1).wait_send()
        for c in chunks:
            along(text, z, 0, middle, c).wait_send()

    @pl.when(is_middle)
    def _():
        beside, over, far = group.at[end], group.at[far_middle], group.at[far_end]
        first, second = images.at[pl.ds(0, 2)], images.at[pl.ds(2, 2)]
        for c in chunks:
            along(text, z, 0, far_middle, c).start()
            along(text, z, 1, end, c).start()
        for c in chunks:
            image_across(image, 0, c).start()
        for c in chunks:
            across(text, z, c).start()
        for load in loads:
            load.wait()
        for c in chunks:
            image_inward(c).wait_recv()
            image_across(images.at[2], 1, c).start()
            along(text, far_middle, 0, middle, c).wait_recv()
            along(over, far_middle, 0, end, c).start()
            across(over, far_middle, c).start()
        for c in chunks:
            image_across(image, 0, c).wait_recv()
        total[2] = pair(over[...], first)
        for c in chunks:
            along(text, end, 0, middle, c).wait_recv()
            along(beside, end, 0, far_middle, c).start()
            across(beside, end, c).start()
            if c == 0:
                total[0] = pair(group[z], first, 0)
            if c == 1:
                add_group(1, 2, (z - 1) * rows, first=True)
        for c in chunks:
            image_across(image, 1, c).wait_recv()
        part_out[0] = (total[2] + pair(over[...], second)).astype(jnp.bfloat16)
        for c in chunks[:AHEAD]:
            part(0, c).start()
        for c in chunks:
            along(text, far_end, 0, middle, c).wait_recv()
            along(far, far_end, 0, end, c).start()
            across(far, far_end, c).start()
        part_out[1] = pair(far[...], images).astype(jnp.bfloat16)
        for c in chunks:
            part(1, c).start()
        total[1] = pair(beside[...], images, 2 * rows)
        total[0] += pair(group[z], second)
        between = (
            lambda: add_group(end, 1),
            lambda: add_group(far_end, 1),
            lambda: add_guest(1, 2),
            lambda: add_guest(end, 1),
        )
        gate = CHUNKS // 2 - 1
        for c in chunks:
            part(1, c).wait_recv()
            row_out[piece(c), :] = (
                total[1, piece(c), :] + part_in[1, piece(c), :].astype(jnp.float32)
            ).astype(jnp.bfloat16)
            row_block(c).start()
            if c == gate:
                for early in chunks[: gate + 1]:
                    part(1, early).wait_send()
                for late in chunks[AHEAD:]:
                    part(0, late).start()
            if c < len(between):
                between[c]()
        add_guest(far_end, 1)
        for c in chunks:
            part(0, c).wait_recv()
            grad_text[piece(c), :] = (
                total[0, piece(c), :] + part_in[0, piece(c), :].astype(jnp.float32)
            )

        for c in chunks[gate + 1 :]:
            part(1, c).wait_send()
        for c in chunks:
            along(text, z, 0, far_middle, c).wait_send()
            along(text, z, 1, end, c).wait_send()
            along(text, end, 0, far_middle, c).wait_send()
            along(text, far_middle, 0, end, c).wait_send()
            along(text, far_end, 0, end, c).wait_send()
            image_across(image, 0, c).wait_send()
            image_across(image, 1, c).wait_send()
            part(0, c).wait_send()
            row_block(c).wait_send()

    for slot in range(4):
        for c in chunks:
            across(text, slot, c).wait_send()


def solution(mesh):
    n, m = mesh.shape["inner"], mesh.shape["outer"]

    def per_device(image, text, scale, offset):
        rows, width = image.shape
        dma = pltpu.SemaphoreType.DMA
        block = (rows, width)
        if n == 4:
            body = functools.partial(line4_kernel, m)
            scratch = [
                pltpu.SMEM((1,), jnp.float32),
                pltpu.SMEM((1,), jnp.float32),
                pltpu.VMEM((4, *block), jnp.bfloat16),
                pltpu.VMEM((4, *block), jnp.bfloat16),
                pltpu.VMEM((4, *block), jnp.bfloat16),
                pltpu.VMEM((3, *block), jnp.float32),
                pltpu.VMEM((2, *block), jnp.bfloat16),
                pltpu.VMEM((2, *block), jnp.bfloat16),
                pltpu.VMEM(block, jnp.bfloat16),
                pltpu.VMEM(block, jnp.bfloat16),
                dma((4,)), dma((4, 2, CHUNKS)), dma((4, CHUNKS)), dma((4, CHUNKS)), dma((4, CHUNKS)),
                dma((CHUNKS,)), dma((CHUNKS,)), dma((2, CHUNKS)), dma((2, CHUNKS)),
                dma((2, CHUNKS)), dma((2, CHUNKS)), dma((CHUNKS,)), dma((CHUNKS,)),
            ]
        else:
            body = functools.partial(kernel, n, m)
            scratch = [
                pltpu.VMEM((2, *block), jnp.bfloat16),
                pltpu.VMEM((2, n, *block), jnp.bfloat16),
                pltpu.VMEM((2, n, *block), jnp.bfloat16),
                dma((2,)), dma((2, n, 2)), dma((2, n)), dma((2, n)), dma((2, n)),
            ]
        return pl.pallas_call(
            body,
            out_shape=(pltpu.VMEM((rows, width), jnp.float32),) * 2,
            in_specs=[pl.BlockSpec(memory_space=pltpu.HBM)] * 2
            + [pl.BlockSpec(memory_space=pltpu.HBM if n == 4 else pltpu.SMEM)] * 2,
            out_specs=(pl.BlockSpec(memory_space=pltpu.VMEM),) * 2,
            scratch_shapes=scratch,
            compiler_params=pltpu.CompilerParams(
                collective_id=0, has_side_effects=True, vmem_limit_bytes=58 * 1024 * 1024
            ),
            cost_estimate=pl.CostEstimate(
                flops=16 * n * rows * rows * width,
                bytes_accessed=12 * rows * width,
                transcendentals=4 * n * rows * rows,
            ),
        )(image, text, scale, offset)

    return jax.shard_map(
        per_device,
        mesh=mesh,
        in_specs=(P(("outer", "inner"), None), P(("outer", "inner"), None), P(), P()),
        out_specs=(P(("outer", "inner"), None), P(("outer", "inner"), None)),
        check_vma=False,
    )
```

```python
import functools

import jax
import jax.numpy as jnp
from jax import lax
from jax.experimental import pallas as pl
from jax.experimental.pallas import tpu as pltpu
from jax.sharding import PartitionSpec as P

MESH = pl.DeviceIdType.MESH
TEXT, IMAGE = 0, 1
CHUNKS = 4


def kernel(
    n, m, image, text, scale, offset, grad_image, grad_text,
    own, group, guest, load_sem, line_send, line_recv, side_send, side_recv,
):
    outer, z = lax.axis_index("outer"), lax.axis_index("inner")
    above, below = lax.rem(outer + 1, m), lax.rem(outer + m - 1, m)
    rows = text.shape[0]
    source = (text, image)
    side = (above, below)

    loads = [pltpu.make_async_copy(source[k], own.at[k], load_sem.at[k]) for k in (TEXT, IMAGE)]
    for load in loads:
        load.start()

    barrier = pltpu.get_barrier_semaphore()

    def greet(o, i):
        pl.semaphore_signal(barrier, inc=1, device_id=(o, i), device_id_type=MESH)

    greet(above, z)
    greet(below, z)
    pl.when(z > 0)(lambda: greet(outer, z - 1))
    pl.when(z < n - 1)(lambda: greet(outer, z + 1))
    pl.semaphore_wait(barrier, 2 + (z > 0).astype(jnp.int32) + (z < n - 1).astype(jnp.int32))

    def along(k, src, slot, way):
        return pltpu.make_async_remote_copy(
            src_ref=src,
            dst_ref=group.at[k, slot],
            send_sem=line_send.at[k, slot, way],
            recv_sem=line_recv.at[k, slot],
            device_id=(outer, z + (1 if way else -1)),
            device_id_type=MESH,
        )

    def across(k, src, slot):
        return pltpu.make_async_remote_copy(
            src_ref=src,
            dst_ref=guest.at[k, slot],
            send_sem=side_send.at[k, slot],
            recv_sem=side_recv.at[k, slot],
            device_id=(side[k], z),
            device_id_type=MESH,
        )

    def has_next(way):
        return z < n - 1 if way else z > 0

    def add(k, block, first=False):
        out = (grad_image, grad_text)[k]
        product = lax.dot_general(
            own[1 - k], block[...], (((1,), (1,)), ((), ())), preferred_element_type=jnp.float32
        )
        logit = scale[0] * product + offset[0]
        if first:
            row = lax.broadcasted_iota(jnp.int32, (rows, rows), 0)
            column = lax.broadcasted_iota(jnp.int32, (rows, rows), 1)
            sign = jnp.where(row == column, 1.0, -1.0)
            coef = -sign * jax.nn.sigmoid(-sign * logit) * scale[0]
        else:
            coef = jax.nn.sigmoid(logit) * scale[0]
        term = jnp.dot(coef.astype(jnp.bfloat16), block[...], preferred_element_type=jnp.float32)
        out[...] = term if first else out[...] + term

    for k in (TEXT, IMAGE):
        for way in (1, 0):
            pl.when(has_next(way))(lambda: along(k, source[k], z, way).start())
        across(k, source[k], z).start()

    for load in loads:
        load.wait()
    for k in (TEXT, IMAGE):
        add(k, own.at[k], first=True)

    def visit(k, slot):
        across(k, guest.at[k, slot], slot).wait_recv()
        add(k, guest.at[k, slot])

    visit(TEXT, z)

    def step(s, _):
        def from_line(k):
            for way in (1, 0):
                slot = z - s if way else z + s

                @pl.when(slot >= 0 if way else slot < n)
                def _():
                    along(k, source[k], slot, way).wait_recv()
                    pl.when(has_next(way))(
                        lambda: along(k, group.at[k, slot], slot, way).start()
                    )
                    across(k, group.at[k, slot], slot).start()

            for way in (1, 0):
                slot = z - s if way else z + s
                pl.when(slot >= 0 if way else slot < n)(lambda: add(k, group.at[k, slot]))

        from_line(TEXT)
        pl.when(z - s + 1 >= 0)(lambda: visit(IMAGE, z - s + 1))
        pl.when((z + s - 1 < n) & (s > 1))(lambda: visit(IMAGE, z + s - 1))
        from_line(IMAGE)
        pl.when(z - s >= 0)(lambda: visit(TEXT, z - s))
        pl.when(z + s < n)(lambda: visit(TEXT, z + s))
        return 0

    lax.fori_loop(1, n, step, 0)
    if n > 1:
        pl.when(z - n + 1 >= 0)(lambda: visit(IMAGE, z - n + 1))
        pl.when(z + n - 1 < n)(lambda: visit(IMAGE, z + n - 1))

    def drain(slot, _):
        for k in (TEXT, IMAGE):
            across(k, source[k], slot).wait_send()
            pl.when((slot <= z) & (z < n - 1))(lambda: along(k, source[k], slot, 1).wait_send())
            pl.when((slot >= z) & (z > 0))(lambda: along(k, source[k], slot, 0).wait_send())
        return 0

    lax.fori_loop(0, n, drain, 0)


def line4_kernel(
    m, image, text, scale, offset, grad_image, grad_text,
    group, guest, images, total, part_out, part_in, row_out, row_in,
    load_sem, line_send, line_recv, side_send, side_recv, image_send, image_recv,
    guest_send, guest_recv, part_send, part_recv, row_send, row_recv,
):
    outer, z = lax.axis_index("outer"), lax.axis_index("inner")
    above, below = lax.rem(outer + 1, m), lax.rem(outer + m - 1, m)
    rows, width = text.shape
    size = rows // CHUNKS
    is_end = (z == 0) | (z == 3)
    is_middle = (z == 1) | (z == 2)
    high = (z >= 2).astype(jnp.int32)
    end, middle = 3 * high, 1 + high
    far_end, far_middle = 3 - end, 3 - middle

    loads = [
        pltpu.make_async_copy(image, images.at[0], load_sem.at[0]),
        pltpu.make_async_copy(text, group.at[z], load_sem.at[1]),
    ]
    for load in loads:
        load.start()

    barrier = pltpu.get_barrier_semaphore()

    def greet(o, i):
        pl.semaphore_signal(barrier, inc=1, device_id=(o, i), device_id_type=MESH)

    greet(above, z)
    greet(below, z)
    pl.when(z > 0)(lambda: greet(outer, z - 1))
    pl.when(z < 3)(lambda: greet(outer, z + 1))
    pl.semaphore_wait(barrier, 2 + (z > 0).astype(jnp.int32) + (z < 3).astype(jnp.int32))

    def remote(src, dst, send, recv, o, i):
        return pltpu.make_async_remote_copy(
            src_ref=src, dst_ref=dst, send_sem=send, recv_sem=recv,
            device_id=(o, i), device_id_type=MESH,
        )

    def piece(c):
        return pl.ds(c * size, size)

    def half(h):
        return pl.ds(h * (rows // 2), rows // 2)

    def along(src, slot, way, to, c):
        return remote(
            src.at[piece(c)], group.at[slot, piece(c)],
            line_send.at[slot, way, c], line_recv.at[slot, c], outer, to,
        )

    def across(src, slot, h):
        return remote(
            src.at[half(h)], guest.at[slot, half(h)],
            side_send.at[slot, h], side_recv.at[slot, h], above, z,
        )

    def across_after(src, slot, c):
        if (c + 1) % (CHUNKS // 2) == 0:
            across(src, slot, c // (CHUNKS // 2)).start()

    def image_inward(c):
        return remote(
            image.at[piece(c)], images.at[2, piece(c)],
            image_send.at[c], image_recv.at[c], outer, middle,
        )

    def image_across(src, i, c):
        return remote(
            src.at[piece(c)], images.at[1 + 2 * i, piece(c)],
            guest_send.at[i, c], guest_recv.at[i, c], below, z,
        )

    def part(i, h):
        return remote(
            part_out.at[i, half(h)], part_in.at[i, half(h)],
            part_send.at[i, h], part_recv.at[i, h], outer, far_middle,
        )

    def row_block(h):
        return remote(
            row_out.at[half(h)], row_in.at[half(h)], row_send.at[h], row_recv.at[h], outer, end
        )

    def weigh(left, right, match=None):
        product = lax.dot_general(
            left, right, (((1,), (1,)), ((), ())), preferred_element_type=jnp.float32
        )
        logit = scale[0] * product + offset[0]
        if match is not None:
            row = lax.broadcasted_iota(jnp.int32, logit.shape, 0)
            column = lax.broadcasted_iota(jnp.int32, logit.shape, 1)
            sign = jnp.where(column == row + match, 1.0, -1.0)
            coef = -sign * jax.nn.sigmoid(-sign * logit) * scale[0]
        else:
            coef = jax.nn.sigmoid(logit) * scale[0]
        return coef.astype(jnp.bfloat16)

    def pair(left, blocks, match=None):
        right = blocks[...].reshape(-1, width)
        coef = weigh(left, right, match)
        return jnp.dot(coef, right, preferred_element_type=jnp.float32)

    def add_group(slot, count, match=None, first=False):
        term = pair(images[0], group.at[pl.ds(slot, count)], match)
        grad_image[...] = term if first else grad_image[...] + term

    def add_guest(slot, count):
        for k in range(count):
            for h in (0, 1):
                across(text, slot + k, h).wait_recv()
        grad_image[...] += pair(images[0], guest.at[pl.ds(slot, count)])

    chunks = range(CHUNKS)

    @pl.when(is_end)
    def _():
        for c in chunks:
            image_inward(c).start()
        for h in (0, 1):
            across(text, z, h).start()
        for load in loads:
            load.wait()
        for c in chunks[:-1]:
            image_inward(c).wait_send()
        for c in chunks:
            along(text, z, 0, middle, c).start()
        add_group(z, 1, 0, first=True)
        for slot in (middle, far_middle, far_end):
            for c in chunks:
                along(text, slot, 0, end, c).wait_recv()
                across_after(group.at[slot], slot, c)
        add_group(1, 2)
        add_group(far_end, 1)
        add_guest(end, 1)
        add_guest(1, 2)
        add_guest(far_end, 1)
        for h in (0, 1):
            row_block(h).wait_recv()
            grad_text[half(h), :] = row_in[half(h), :].astype(jnp.float32)
        image_inward(CHUNKS - 1).wait_send()
        for c in chunks:
            along(text, z, 0, middle, c).wait_send()

    @pl.when(is_middle)
    def _():
        beside, over, far = group.at[end], group.at[far_middle], group.at[far_end]
        first, second = images.at[pl.ds(0, 2)], images.at[pl.ds(2, 2)]
        for c in chunks:
            along(text, z, 0, far_middle, c).start()
            along(text, z, 1, end, c).start()
        for c in chunks:
            image_across(image, 0, c).start()
        for h in (0, 1):
            across(text, z, h).start()
        for load in loads:
            load.wait()
        for c in chunks:
            image_inward(c).wait_recv()
            image_across(images.at[2], 1, c).start()
            along(text, far_middle, 0, middle, c).wait_recv()
            along(over, far_middle, 0, end, c).start()
            across_after(over, far_middle, c)
        for c in chunks:
            image_across(image, 0, c).wait_recv()
        total[2] = pair(over[...], first)
        for c in chunks:
            along(text, end, 0, middle, c).wait_recv()
            along(beside, end, 0, far_middle, c).start()
            across_after(beside, end, c)
            if c == 0:
                total[0] = pair(group[z], first, 0)
            if c == 1:
                add_group(1, 2, (z - 1) * rows, first=True)
        for c in chunks:
            image_across(image, 1, c).wait_recv()
        part_out[0] = (total[2] + pair(over[...], second)).astype(jnp.bfloat16)
        part(0, 0).start()
        for c in chunks:
            along(text, far_end, 0, middle, c).wait_recv()
            along(far, far_end, 0, end, c).start()
            across_after(far, far_end, c)
        part_out[1] = pair(far[...], images).astype(jnp.bfloat16)
        for h in (0, 1):
            part(1, h).start()
        total[1] = pair(beside[...], images, 2 * rows)
        total[0] += pair(group[z], second)
        for h in (0, 1):
            part(1, h).wait_recv()
            row_out[half(h), :] = (
                total[1, half(h), :] + part_in[1, half(h), :].astype(jnp.float32)
            ).astype(jnp.bfloat16)
            row_block(h).start()
            if h == 0:
                part(1, 0).wait_send()
                part(0, 1).start()
                add_group(end, 1)
                add_group(far_end, 1)
        add_guest(1, 2)
        add_guest(end, 1)
        add_guest(far_end, 1)
        for h in (0, 1):
            part(0, h).wait_recv()
            grad_text[half(h), :] = (
                total[0, half(h), :] + part_in[0, half(h), :].astype(jnp.float32)
            )

        part(1, 1).wait_send()
        for h in (0, 1):
            part(0, h).wait_send()
            row_block(h).wait_send()
        for c in chunks:
            along(text, z, 0, far_middle, c).wait_send()
            along(text, z, 1, end, c).wait_send()
            along(text, end, 0, far_middle, c).wait_send()
            along(text, far_middle, 0, end, c).wait_send()
            along(text, far_end, 0, end, c).wait_send()
            image_across(image, 0, c).wait_send()
            image_across(image, 1, c).wait_send()

    for slot in range(4):
        for h in (0, 1):
            across(text, slot, h).wait_send()


def solution(mesh):
    n, m = mesh.shape["inner"], mesh.shape["outer"]

    def per_device(image, text, scale, offset):
        rows, width = image.shape
        dma = pltpu.SemaphoreType.DMA
        block = (rows, width)
        if n == 4:
            body = functools.partial(line4_kernel, m)
            scratch = [
                pltpu.VMEM((4, *block), jnp.bfloat16),
                pltpu.VMEM((4, *block), jnp.bfloat16),
                pltpu.VMEM((4, *block), jnp.bfloat16),
                pltpu.VMEM((3, *block), jnp.float32),
                pltpu.VMEM((2, *block), jnp.bfloat16),
                pltpu.VMEM((2, *block), jnp.bfloat16),
                pltpu.VMEM(block, jnp.bfloat16),
                pltpu.VMEM(block, jnp.bfloat16),
                dma((2,)), dma((4, 2, CHUNKS)), dma((4, CHUNKS)), dma((4, 2)), dma((4, 2)),
                dma((CHUNKS,)), dma((CHUNKS,)), dma((2, CHUNKS)), dma((2, CHUNKS)),
                dma((2, 2)), dma((2, 2)), dma((2,)), dma((2,)),
            ]
        else:
            body = functools.partial(kernel, n, m)
            scratch = [
                pltpu.VMEM((2, *block), jnp.bfloat16),
                pltpu.VMEM((2, n, *block), jnp.bfloat16),
                pltpu.VMEM((2, n, *block), jnp.bfloat16),
                dma((2,)), dma((2, n, 2)), dma((2, n)), dma((2, n)), dma((2, n)),
            ]
        return pl.pallas_call(
            body,
            out_shape=(pltpu.VMEM((rows, width), jnp.float32),) * 2,
            in_specs=[pl.BlockSpec(memory_space=pltpu.HBM)] * 2
            + [pl.BlockSpec(memory_space=pltpu.SMEM)] * 2,
            out_specs=(pl.BlockSpec(memory_space=pltpu.VMEM),) * 2,
            scratch_shapes=scratch,
            compiler_params=pltpu.CompilerParams(
                collective_id=0, has_side_effects=True, vmem_limit_bytes=58 * 1024 * 1024
            ),
            cost_estimate=pl.CostEstimate(
                flops=16 * n * rows * rows * width,
                bytes_accessed=12 * rows * width,
                transcendentals=4 * n * rows * rows,
            ),
        )(image, text, scale, offset)

    return jax.shard_map(
        per_device,
        mesh=mesh,
        in_specs=(P(("outer", "inner"), None), P(("outer", "inner"), None), P(), P()),
        out_specs=(P(("outer", "inner"), None), P(("outer", "inner"), None)),
        check_vma=False,
    )
```

```python
import functools

import jax
import jax.numpy as jnp
from jax import lax
from jax.experimental import pallas as pl
from jax.experimental.pallas import tpu as pltpu
from jax.sharding import PartitionSpec as P

MESH = pl.DeviceIdType.MESH
TEXT, IMAGE = 0, 1
CHUNKS = 4


def kernel(
    n, m, image, text, scale, offset, grad_image, grad_text,
    own, group, guest, load_sem, line_send, line_recv, side_send, side_recv,
):
    outer, z = lax.axis_index("outer"), lax.axis_index("inner")
    above, below = lax.rem(outer + 1, m), lax.rem(outer + m - 1, m)
    rows = text.shape[0]
    source = (text, image)
    side = (above, below)

    loads = [pltpu.make_async_copy(source[k], own.at[k], load_sem.at[k]) for k in (TEXT, IMAGE)]
    for load in loads:
        load.start()

    barrier = pltpu.get_barrier_semaphore()

    def greet(o, i):
        pl.semaphore_signal(barrier, inc=1, device_id=(o, i), device_id_type=MESH)

    greet(above, z)
    greet(below, z)
    pl.when(z > 0)(lambda: greet(outer, z - 1))
    pl.when(z < n - 1)(lambda: greet(outer, z + 1))
    pl.semaphore_wait(barrier, 2 + (z > 0).astype(jnp.int32) + (z < n - 1).astype(jnp.int32))

    def along(k, src, slot, way):
        return pltpu.make_async_remote_copy(
            src_ref=src,
            dst_ref=group.at[k, slot],
            send_sem=line_send.at[k, slot, way],
            recv_sem=line_recv.at[k, slot],
            device_id=(outer, z + (1 if way else -1)),
            device_id_type=MESH,
        )

    def across(k, src, slot):
        return pltpu.make_async_remote_copy(
            src_ref=src,
            dst_ref=guest.at[k, slot],
            send_sem=side_send.at[k, slot],
            recv_sem=side_recv.at[k, slot],
            device_id=(side[k], z),
            device_id_type=MESH,
        )

    def has_next(way):
        return z < n - 1 if way else z > 0

    def add(k, block, first=False):
        out = (grad_image, grad_text)[k]
        product = lax.dot_general(
            own[1 - k], block[...], (((1,), (1,)), ((), ())), preferred_element_type=jnp.float32
        )
        logit = scale[0] * product + offset[0]
        if first:
            row = lax.broadcasted_iota(jnp.int32, (rows, rows), 0)
            column = lax.broadcasted_iota(jnp.int32, (rows, rows), 1)
            sign = jnp.where(row == column, 1.0, -1.0)
            coef = -sign * jax.nn.sigmoid(-sign * logit) * scale[0]
        else:
            coef = jax.nn.sigmoid(logit) * scale[0]
        term = jnp.dot(coef.astype(jnp.bfloat16), block[...], preferred_element_type=jnp.float32)
        out[...] = term if first else out[...] + term

    for k in (TEXT, IMAGE):
        for way in (1, 0):
            pl.when(has_next(way))(lambda: along(k, source[k], z, way).start())
        across(k, source[k], z).start()

    for load in loads:
        load.wait()
    for k in (TEXT, IMAGE):
        add(k, own.at[k], first=True)

    def visit(k, slot):
        across(k, guest.at[k, slot], slot).wait_recv()
        add(k, guest.at[k, slot])

    visit(TEXT, z)

    def step(s, _):
        def from_line(k):
            for way in (1, 0):
                slot = z - s if way else z + s

                @pl.when(slot >= 0 if way else slot < n)
                def _():
                    along(k, source[k], slot, way).wait_recv()
                    pl.when(has_next(way))(
                        lambda: along(k, group.at[k, slot], slot, way).start()
                    )
                    across(k, group.at[k, slot], slot).start()

            for way in (1, 0):
                slot = z - s if way else z + s
                pl.when(slot >= 0 if way else slot < n)(lambda: add(k, group.at[k, slot]))

        from_line(TEXT)
        pl.when(z - s + 1 >= 0)(lambda: visit(IMAGE, z - s + 1))
        pl.when((z + s - 1 < n) & (s > 1))(lambda: visit(IMAGE, z + s - 1))
        from_line(IMAGE)
        pl.when(z - s >= 0)(lambda: visit(TEXT, z - s))
        pl.when(z + s < n)(lambda: visit(TEXT, z + s))
        return 0

    lax.fori_loop(1, n, step, 0)
    if n > 1:
        pl.when(z - n + 1 >= 0)(lambda: visit(IMAGE, z - n + 1))
        pl.when(z + n - 1 < n)(lambda: visit(IMAGE, z + n - 1))

    def drain(slot, _):
        for k in (TEXT, IMAGE):
            across(k, source[k], slot).wait_send()
            pl.when((slot <= z) & (z < n - 1))(lambda: along(k, source[k], slot, 1).wait_send())
            pl.when((slot >= z) & (z > 0))(lambda: along(k, source[k], slot, 0).wait_send())
        return 0

    lax.fori_loop(0, n, drain, 0)


def line4_kernel(
    m, image, text, scale, offset, grad_image, grad_text,
    group, guest, images, total, part_out, part_in, row_out, row_in,
    load_sem, line_send, line_recv, side_send, side_recv, image_send, image_recv,
    guest_send, guest_recv, part_send, part_recv, row_send, row_recv, turn,
):
    outer, z = lax.axis_index("outer"), lax.axis_index("inner")
    above, below = lax.rem(outer + 1, m), lax.rem(outer + m - 1, m)
    rows, width = text.shape
    size = rows // CHUNKS
    is_end = (z == 0) | (z == 3)
    is_middle = (z == 1) | (z == 2)
    high = (z >= 2).astype(jnp.int32)
    end, middle = 3 * high, 1 + high
    far_end, far_middle = 3 - end, 3 - middle

    loads = [
        pltpu.make_async_copy(image, images.at[0], load_sem.at[0]),
        pltpu.make_async_copy(text, group.at[z], load_sem.at[1]),
    ]
    for load in loads:
        load.start()

    barrier = pltpu.get_barrier_semaphore()

    def greet(o, i):
        pl.semaphore_signal(barrier, inc=1, device_id=(o, i), device_id_type=MESH)

    greet(above, z)
    greet(below, z)
    pl.when(z > 0)(lambda: greet(outer, z - 1))
    pl.when(z < 3)(lambda: greet(outer, z + 1))
    pl.semaphore_wait(barrier, 2 + (z > 0).astype(jnp.int32) + (z < 3).astype(jnp.int32))

    def remote(src, dst, send, recv, o, i):
        return pltpu.make_async_remote_copy(
            src_ref=src, dst_ref=dst, send_sem=send, recv_sem=recv,
            device_id=(o, i), device_id_type=MESH,
        )

    def piece(c):
        return pl.ds(c * size, size)

    def along(src, slot, way, to, c):
        return remote(
            src.at[piece(c)], group.at[slot, piece(c)],
            line_send.at[slot, way, c], line_recv.at[slot, c], outer, to,
        )

    def across(src, slot, c):
        return remote(
            src.at[piece(c)], guest.at[slot, piece(c)],
            side_send.at[slot, c], side_recv.at[slot, c], above, z,
        )

    def image_inward(c):
        return remote(
            image.at[piece(c)], images.at[2, piece(c)],
            image_send.at[c], image_recv.at[c], outer, middle,
        )

    def image_across(src, i, c):
        return remote(
            src.at[piece(c)], images.at[1 + 2 * i, piece(c)],
            guest_send.at[i, c], guest_recv.at[i, c], below, z,
        )

    def part(i, c):
        return remote(
            part_out.at[i, piece(c)], part_in.at[i, piece(c)],
            part_send.at[i, c], part_recv.at[i, c], outer, far_middle,
        )

    def row_block(c):
        return remote(
            row_out.at[piece(c)], row_in.at[piece(c)], row_send.at[c], row_recv.at[c], outer, end
        )

    def weigh(left, right, match=None):
        product = lax.dot_general(
            left, right, (((1,), (1,)), ((), ())), preferred_element_type=jnp.float32
        )
        logit = scale[0] * product + offset[0]
        if match is not None:
            row = lax.broadcasted_iota(jnp.int32, logit.shape, 0)
            column = lax.broadcasted_iota(jnp.int32, logit.shape, 1)
            sign = jnp.where(column == row + match, 1.0, -1.0)
            coef = -sign * jax.nn.sigmoid(-sign * logit) * scale[0]
        else:
            coef = jax.nn.sigmoid(logit) * scale[0]
        return coef.astype(jnp.bfloat16)

    def pair(left, blocks, match=None):
        right = blocks[...].reshape(-1, width)
        coef = weigh(left, right, match)
        return jnp.dot(coef, right, preferred_element_type=jnp.float32)

    def add_group(slot, count, match=None, first=False):
        term = pair(images[0], group.at[pl.ds(slot, count)], match)
        grad_image[...] = term if first else grad_image[...] + term

    def add_guest(slot, count):
        for k in range(count):
            for c in chunks:
                across(text, slot + k, c).wait_recv()
        grad_image[...] += pair(images[0], guest.at[pl.ds(slot, count)])

    chunks = range(CHUNKS)

    @pl.when(is_end)
    def _():
        for c in chunks:
            along(text, z, 0, middle, c).start()
        for c in chunks:
            across(text, z, c).start()
        for c in chunks[:-1]:
            along(text, z, 0, middle, c).wait_send()
        odd = lax.rem(outer, 2) == 1
        pl.when(odd)(lambda: pl.semaphore_wait(turn, 1))
        for c in chunks:
            image_inward(c).start()
        for c in chunks[:-1]:
            image_inward(c).wait_send()
        pl.when(jnp.logical_not(odd) & (outer + 1 < m))(
            lambda: pl.semaphore_signal(
                turn, inc=1, device_id=(above, z), device_id_type=MESH
            )
        )
        for load in loads:
            load.wait()
        add_group(z, 1, 0, first=True)
        for slot in (middle, far_middle, far_end):
            for c in chunks:
                along(text, slot, 0, end, c).wait_recv()
                across(group.at[slot], slot, c).start()
        add_group(1, 2)
        add_group(far_end, 1)
        add_guest(end, 1)
        add_guest(1, 2)
        add_guest(far_end, 1)
        for c in chunks:
            row_block(c).wait_recv()
            grad_text[piece(c), :] = row_in[piece(c), :].astype(jnp.float32)
        image_inward(CHUNKS - 1).wait_send()
        along(text, z, 0, middle, CHUNKS - 1).wait_send()

    @pl.when(is_middle)
    def _():
        beside, over, far = group.at[end], group.at[far_middle], group.at[far_end]
        first, second = images.at[pl.ds(0, 2)], images.at[pl.ds(2, 2)]
        for c in chunks:
            along(text, z, 0, far_middle, c).start()
            along(text, z, 1, end, c).start()
        for c in chunks:
            image_across(image, 0, c).start()
        for c in chunks:
            across(text, z, c).start()
        for load in loads:
            load.wait()
        for c in chunks:
            along(text, end, 0, middle, c).wait_recv()
            along(beside, end, 0, far_middle, c).start()
            across(beside, end, c).start()
        for c in chunks:
            along(text, far_middle, 0, middle, c).wait_recv()
            along(over, far_middle, 0, end, c).start()
            across(over, far_middle, c).start()
        for c in chunks:
            image_across(image, 0, c).wait_recv()
        total[2] = pair(over[...], first)
        total[1] = pair(beside[...], first)
        for c in chunks:
            image_inward(c).wait_recv()
            image_across(images.at[2], 1, c).start()
            if c == 0:
                total[0] = pair(group[z], first, 0)
        for c in chunks:
            along(text, far_end, 0, middle, c).wait_recv()
            along(far, far_end, 0, end, c).start()
            across(far, far_end, c).start()
        for c in chunks:
            image_across(image, 1, c).wait_recv()
        part_out[1] = pair(far[...], images).astype(jnp.bfloat16)
        for c in chunks:
            part(1, c).start()
        part_out[0] = (total[2] + pair(over[...], second)).astype(jnp.bfloat16)
        total[1] += pair(beside[...], second, 0)
        total[0] += pair(group[z], second)
        between = (
            lambda: add_group(1, 2, (z - 1) * rows, first=True),
            lambda: add_group(end, 1),
            lambda: add_group(far_end, 1),
            lambda: add_guest(1, 2),
        )
        gate = CHUNKS - 2
        for c in chunks:
            part(1, c).wait_recv()
            row_out[piece(c), :] = (
                total[1, piece(c), :] + part_in[1, piece(c), :].astype(jnp.float32)
            ).astype(jnp.bfloat16)
            row_block(c).start()
            if c == gate:
                for early in chunks[: gate + 1]:
                    part(1, early).wait_send()
                for late in chunks:
                    part(0, late).start()
            if c < len(between):
                between[c]()
        add_guest(end, 1)
        add_guest(far_end, 1)
        for c in chunks:
            part(0, c).wait_recv()
            grad_text[piece(c), :] = (
                total[0, piece(c), :] + part_in[0, piece(c), :].astype(jnp.float32)
            )

        for c in chunks[gate + 1 :]:
            part(1, c).wait_send()
        for c in chunks:
            along(text, z, 0, far_middle, c).wait_send()
            along(text, z, 1, end, c).wait_send()
            along(text, end, 0, far_middle, c).wait_send()
            along(text, far_middle, 0, end, c).wait_send()
            along(text, far_end, 0, end, c).wait_send()
            image_across(image, 0, c).wait_send()
            image_across(image, 1, c).wait_send()
            part(0, c).wait_send()
            row_block(c).wait_send()

    for slot in range(4):
        for c in chunks:
            across(text, slot, c).wait_send()


def solution(mesh):
    n, m = mesh.shape["inner"], mesh.shape["outer"]

    def per_device(image, text, scale, offset):
        rows, width = image.shape
        dma = pltpu.SemaphoreType.DMA
        block = (rows, width)
        if n == 4:
            body = functools.partial(line4_kernel, m)
            scratch = [
                pltpu.VMEM((4, *block), jnp.bfloat16),
                pltpu.VMEM((4, *block), jnp.bfloat16),
                pltpu.VMEM((4, *block), jnp.bfloat16),
                pltpu.VMEM((3, *block), jnp.float32),
                pltpu.VMEM((2, *block), jnp.bfloat16),
                pltpu.VMEM((2, *block), jnp.bfloat16),
                pltpu.VMEM(block, jnp.bfloat16),
                pltpu.VMEM(block, jnp.bfloat16),
                dma((2,)), dma((4, 2, CHUNKS)), dma((4, CHUNKS)), dma((4, CHUNKS)), dma((4, CHUNKS)),
                dma((CHUNKS,)), dma((CHUNKS,)), dma((2, CHUNKS)), dma((2, CHUNKS)),
                dma((2, CHUNKS)), dma((2, CHUNKS)), dma((CHUNKS,)), dma((CHUNKS,)),
                pltpu.SemaphoreType.REGULAR,
            ]
        else:
            body = functools.partial(kernel, n, m)
            scratch = [
                pltpu.VMEM((2, *block), jnp.bfloat16),
                pltpu.VMEM((2, n, *block), jnp.bfloat16),
                pltpu.VMEM((2, n, *block), jnp.bfloat16),
                dma((2,)), dma((2, n, 2)), dma((2, n)), dma((2, n)), dma((2, n)),
            ]
        return pl.pallas_call(
            body,
            out_shape=(pltpu.VMEM((rows, width), jnp.float32),) * 2,
            in_specs=[pl.BlockSpec(memory_space=pltpu.HBM)] * 2
            + [pl.BlockSpec(memory_space=pltpu.SMEM)] * 2,
            out_specs=(pl.BlockSpec(memory_space=pltpu.VMEM),) * 2,
            scratch_shapes=scratch,
            compiler_params=pltpu.CompilerParams(
                collective_id=0, has_side_effects=True, vmem_limit_bytes=58 * 1024 * 1024
            ),
            cost_estimate=pl.CostEstimate(
                flops=16 * n * rows * rows * width,
                bytes_accessed=12 * rows * width,
                transcendentals=4 * n * rows * rows,
            ),
        )(image, text, scale, offset)

    return jax.shard_map(
        per_device,
        mesh=mesh,
        in_specs=(P(("outer", "inner"), None), P(("outer", "inner"), None), P(), P()),
        out_specs=(P(("outer", "inner"), None), P(("outer", "inner"), None)),
        check_vma=False,
    )
```

```python
import functools

import jax
import jax.numpy as jnp
from jax import lax
from jax.experimental import pallas as pl
from jax.experimental.pallas import tpu as pltpu
from jax.sharding import PartitionSpec as P

MESH = pl.DeviceIdType.MESH
TEXT, IMAGE = 0, 1
CHUNKS = 4


def kernel(
    n, m, image, text, scale, offset, grad_image, grad_text,
    own, group, guest, load_sem, line_send, line_recv, side_send, side_recv,
):
    outer, z = lax.axis_index("outer"), lax.axis_index("inner")
    above, below = lax.rem(outer + 1, m), lax.rem(outer + m - 1, m)
    rows = text.shape[0]
    source = (text, image)
    side = (above, below)

    loads = [pltpu.make_async_copy(source[k], own.at[k], load_sem.at[k]) for k in (TEXT, IMAGE)]
    for load in loads:
        load.start()

    barrier = pltpu.get_barrier_semaphore()

    def greet(o, i):
        pl.semaphore_signal(barrier, inc=1, device_id=(o, i), device_id_type=MESH)

    greet(above, z)
    greet(below, z)
    pl.when(z > 0)(lambda: greet(outer, z - 1))
    pl.when(z < n - 1)(lambda: greet(outer, z + 1))
    pl.semaphore_wait(barrier, 2 + (z > 0).astype(jnp.int32) + (z < n - 1).astype(jnp.int32))

    def along(k, src, slot, way):
        return pltpu.make_async_remote_copy(
            src_ref=src,
            dst_ref=group.at[k, slot],
            send_sem=line_send.at[k, slot, way],
            recv_sem=line_recv.at[k, slot],
            device_id=(outer, z + (1 if way else -1)),
            device_id_type=MESH,
        )

    def across(k, src, slot):
        return pltpu.make_async_remote_copy(
            src_ref=src,
            dst_ref=guest.at[k, slot],
            send_sem=side_send.at[k, slot],
            recv_sem=side_recv.at[k, slot],
            device_id=(side[k], z),
            device_id_type=MESH,
        )

    def has_next(way):
        return z < n - 1 if way else z > 0

    def add(k, block, first=False):
        out = (grad_image, grad_text)[k]
        product = lax.dot_general(
            own[1 - k], block[...], (((1,), (1,)), ((), ())), preferred_element_type=jnp.float32
        )
        logit = scale[0] * product + offset[0]
        if first:
            row = lax.broadcasted_iota(jnp.int32, (rows, rows), 0)
            column = lax.broadcasted_iota(jnp.int32, (rows, rows), 1)
            sign = jnp.where(row == column, 1.0, -1.0)
            coef = -sign * jax.nn.sigmoid(-sign * logit) * scale[0]
        else:
            coef = jax.nn.sigmoid(logit) * scale[0]
        term = jnp.dot(coef.astype(jnp.bfloat16), block[...], preferred_element_type=jnp.float32)
        out[...] = term if first else out[...] + term

    for k in (TEXT, IMAGE):
        for way in (1, 0):
            pl.when(has_next(way))(lambda: along(k, source[k], z, way).start())
        across(k, source[k], z).start()

    for load in loads:
        load.wait()
    for k in (TEXT, IMAGE):
        add(k, own.at[k], first=True)

    def visit(k, slot):
        across(k, guest.at[k, slot], slot).wait_recv()
        add(k, guest.at[k, slot])

    visit(TEXT, z)

    def step(s, _):
        def from_line(k):
            for way in (1, 0):
                slot = z - s if way else z + s

                @pl.when(slot >= 0 if way else slot < n)
                def _():
                    along(k, source[k], slot, way).wait_recv()
                    pl.when(has_next(way))(
                        lambda: along(k, group.at[k, slot], slot, way).start()
                    )
                    across(k, group.at[k, slot], slot).start()

            for way in (1, 0):
                slot = z - s if way else z + s
                pl.when(slot >= 0 if way else slot < n)(lambda: add(k, group.at[k, slot]))

        from_line(TEXT)
        pl.when(z - s + 1 >= 0)(lambda: visit(IMAGE, z - s + 1))
        pl.when((z + s - 1 < n) & (s > 1))(lambda: visit(IMAGE, z + s - 1))
        from_line(IMAGE)
        pl.when(z - s >= 0)(lambda: visit(TEXT, z - s))
        pl.when(z + s < n)(lambda: visit(TEXT, z + s))
        return 0

    lax.fori_loop(1, n, step, 0)
    if n > 1:
        pl.when(z - n + 1 >= 0)(lambda: visit(IMAGE, z - n + 1))
        pl.when(z + n - 1 < n)(lambda: visit(IMAGE, z + n - 1))

    def drain(slot, _):
        for k in (TEXT, IMAGE):
            across(k, source[k], slot).wait_send()
            pl.when((slot <= z) & (z < n - 1))(lambda: along(k, source[k], slot, 1).wait_send())
            pl.when((slot >= z) & (z > 0))(lambda: along(k, source[k], slot, 0).wait_send())
        return 0

    lax.fori_loop(0, n, drain, 0)


def line4_kernel(
    m, image, text, scale, offset, grad_image, grad_text,
    group, guest, images, total, part_out, part_in, row_out, row_in,
    load_sem, line_send, line_recv, side_send, side_recv, image_send, image_recv,
    guest_send, guest_recv, part_send, part_recv, row_send, row_recv, turn,
):
    outer, z = lax.axis_index("outer"), lax.axis_index("inner")
    above, below = lax.rem(outer + 1, m), lax.rem(outer + m - 1, m)
    rows, width = text.shape
    size = rows // CHUNKS
    is_end = (z == 0) | (z == 3)
    is_middle = (z == 1) | (z == 2)
    high = (z >= 2).astype(jnp.int32)
    end, middle = 3 * high, 1 + high
    far_end, far_middle = 3 - end, 3 - middle

    loads = [
        pltpu.make_async_copy(image, images.at[0], load_sem.at[0]),
        pltpu.make_async_copy(text, group.at[z], load_sem.at[1]),
    ]
    for load in loads:
        load.start()

    barrier = pltpu.get_barrier_semaphore()

    def greet(o, i):
        pl.semaphore_signal(barrier, inc=1, device_id=(o, i), device_id_type=MESH)

    greet(above, z)
    greet(below, z)
    pl.when(z > 0)(lambda: greet(outer, z - 1))
    pl.when(z < 3)(lambda: greet(outer, z + 1))
    pl.semaphore_wait(barrier, 2 + (z > 0).astype(jnp.int32) + (z < 3).astype(jnp.int32))

    def remote(src, dst, send, recv, o, i):
        return pltpu.make_async_remote_copy(
            src_ref=src, dst_ref=dst, send_sem=send, recv_sem=recv,
            device_id=(o, i), device_id_type=MESH,
        )

    def piece(c):
        return pl.ds(c * size, size)

    def along(src, slot, way, to, c):
        return remote(
            src.at[piece(c)], group.at[slot, piece(c)],
            line_send.at[slot, way, c], line_recv.at[slot, c], outer, to,
        )

    def across(src, slot, c):
        return remote(
            src.at[piece(c)], guest.at[slot, piece(c)],
            side_send.at[slot, c], side_recv.at[slot, c], above, z,
        )

    def image_inward(c):
        return remote(
            image.at[piece(c)], images.at[2, piece(c)],
            image_send.at[c], image_recv.at[c], outer, middle,
        )

    def image_across(src, i, c):
        return remote(
            src.at[piece(c)], images.at[1 + 2 * i, piece(c)],
            guest_send.at[i, c], guest_recv.at[i, c], below, z,
        )

    def part(i, c):
        return remote(
            part_out.at[i, piece(c)], part_in.at[i, piece(c)],
            part_send.at[i, c], part_recv.at[i, c], outer, far_middle,
        )

    def row_block(c):
        return remote(
            row_out.at[piece(c)], row_in.at[piece(c)], row_send.at[c], row_recv.at[c], outer, end
        )

    def weigh(left, right, match=None):
        product = lax.dot_general(
            left, right, (((1,), (1,)), ((), ())), preferred_element_type=jnp.float32
        )
        logit = scale[0] * product + offset[0]
        if match is not None:
            row = lax.broadcasted_iota(jnp.int32, logit.shape, 0)
            column = lax.broadcasted_iota(jnp.int32, logit.shape, 1)
            sign = jnp.where(column == row + match, 1.0, -1.0)
            coef = -sign * jax.nn.sigmoid(-sign * logit) * scale[0]
        else:
            coef = jax.nn.sigmoid(logit) * scale[0]
        return coef.astype(jnp.bfloat16)

    def pair(left, blocks, match=None):
        right = blocks[...].reshape(-1, width)
        coef = weigh(left, right, match)
        return jnp.dot(coef, right, preferred_element_type=jnp.float32)

    def add_group(slot, count, match=None, first=False):
        term = pair(images[0], group.at[pl.ds(slot, count)], match)
        grad_image[...] = term if first else grad_image[...] + term

    def add_guest(slot, count):
        for k in range(count):
            for c in chunks:
                across(text, slot + k, c).wait_recv()
        grad_image[...] += pair(images[0], guest.at[pl.ds(slot, count)])

    chunks = range(CHUNKS)

    @pl.when(is_end)
    def _():
        for c in chunks:
            along(text, z, 0, middle, c).start()
        for c in chunks:
            across(text, z, c).start()
        for c in chunks[:-1]:
            along(text, z, 0, middle, c).wait_send()
        odd = lax.rem(outer, 2) == 1
        pl.when(odd)(lambda: pl.semaphore_wait(turn, 1))
        for c in chunks:
            image_inward(c).start()
        for c in chunks[:-1]:
            image_inward(c).wait_send()
        pl.when(jnp.logical_not(odd) & (outer + 1 < m))(
            lambda: pl.semaphore_signal(
                turn, inc=1, device_id=(above, z), device_id_type=MESH
            )
        )
        for load in loads:
            load.wait()
        add_group(z, 1, 0, first=True)
        for slot in (middle, far_middle, far_end):
            for c in chunks:
                along(text, slot, 0, end, c).wait_recv()
                across(group.at[slot], slot, c).start()
        add_group(1, 2)
        add_group(far_end, 1)
        add_guest(end, 1)
        add_guest(1, 2)
        add_guest(far_end, 1)
        for c in chunks:
            row_block(c).wait_recv()
            grad_text[piece(c), :] = row_in[piece(c), :].astype(jnp.float32)
        image_inward(CHUNKS - 1).wait_send()
        along(text, z, 0, middle, CHUNKS - 1).wait_send()

    @pl.when(is_middle)
    def _():
        beside, over, far = group.at[end], group.at[far_middle], group.at[far_end]
        first, second = images.at[pl.ds(0, 2)], images.at[pl.ds(2, 2)]
        for c in chunks:
            along(text, z, 0, far_middle, c).start()
            along(text, z, 1, end, c).start()
        for c in chunks:
            image_across(image, 0, c).start()
        for c in chunks:
            across(text, z, c).start()
        for load in loads:
            load.wait()
        for c in chunks:
            along(text, end, 0, middle, c).wait_recv()
            along(beside, end, 0, far_middle, c).start()
            across(beside, end, c).start()
        for c in chunks:
            along(text, far_middle, 0, middle, c).wait_recv()
            along(over, far_middle, 0, end, c).start()
            across(over, far_middle, c).start()
        for c in chunks:
            image_across(image, 0, c).wait_recv()
        total[2] = pair(over[...], first)
        total[1] = pair(beside[...], first)
        for c in chunks:
            image_inward(c).wait_recv()
            image_across(images.at[2], 1, c).start()
            if c == 0:
                total[0] = pair(group[z], first, 0)
        for c in chunks:
            along(text, far_end, 0, middle, c).wait_recv()
            along(far, far_end, 0, end, c).start()
            across(far, far_end, c).start()
        for c in chunks:
            image_across(image, 1, c).wait_recv()
        part_out[1] = pair(far[...], images).astype(jnp.bfloat16)
        for c in chunks:
            part(1, c).start()
        part_out[0] = (total[2] + pair(over[...], second)).astype(jnp.bfloat16)
        total[1] += pair(beside[...], second, 0)
        total[0] += pair(group[z], second)
        between = (
            lambda: add_group(1, 2, (z - 1) * rows, first=True),
            lambda: add_group(end, 1),
            lambda: add_group(far_end, 1),
            lambda: add_guest(1, 2),
        )
        gate = 0
        for c in chunks:
            part(1, c).wait_recv()
            row_out[piece(c), :] = (
                total[1, piece(c), :] + part_in[1, piece(c), :].astype(jnp.float32)
            ).astype(jnp.bfloat16)
            row_block(c).start()
            if c == gate:
                for early in chunks[: gate + 1]:
                    part(1, early).wait_send()
                for late in chunks:
                    part(0, late).start()
            if c < len(between):
                between[c]()
        add_guest(end, 1)
        add_guest(far_end, 1)
        for c in chunks:
            part(0, c).wait_recv()
            grad_text[piece(c), :] = (
                total[0, piece(c), :] + part_in[0, piece(c), :].astype(jnp.float32)
            )

        for c in chunks[gate + 1 :]:
            part(1, c).wait_send()
        for c in chunks:
            along(text, z, 0, far_middle, c).wait_send()
            along(text, z, 1, end, c).wait_send()
            along(text, end, 0, far_middle, c).wait_send()
            along(text, far_middle, 0, end, c).wait_send()
            along(text, far_end, 0, end, c).wait_send()
            image_across(image, 0, c).wait_send()
            image_across(image, 1, c).wait_send()
            part(0, c).wait_send()
            row_block(c).wait_send()

    for slot in range(4):
        for c in chunks:
            across(text, slot, c).wait_send()


def solution(mesh):
    n, m = mesh.shape["inner"], mesh.shape["outer"]

    def per_device(image, text, scale, offset):
        rows, width = image.shape
        dma = pltpu.SemaphoreType.DMA
        block = (rows, width)
        if n == 4:
            body = functools.partial(line4_kernel, m)
            scratch = [
                pltpu.VMEM((4, *block), jnp.bfloat16),
                pltpu.VMEM((4, *block), jnp.bfloat16),
                pltpu.VMEM((4, *block), jnp.bfloat16),
                pltpu.VMEM((3, *block), jnp.float32),
                pltpu.VMEM((2, *block), jnp.bfloat16),
                pltpu.VMEM((2, *block), jnp.bfloat16),
                pltpu.VMEM(block, jnp.bfloat16),
                pltpu.VMEM(block, jnp.bfloat16),
                dma((2,)), dma((4, 2, CHUNKS)), dma((4, CHUNKS)), dma((4, CHUNKS)), dma((4, CHUNKS)),
                dma((CHUNKS,)), dma((CHUNKS,)), dma((2, CHUNKS)), dma((2, CHUNKS)),
                dma((2, CHUNKS)), dma((2, CHUNKS)), dma((CHUNKS,)), dma((CHUNKS,)),
                pltpu.SemaphoreType.REGULAR,
            ]
        else:
            body = functools.partial(kernel, n, m)
            scratch = [
                pltpu.VMEM((2, *block), jnp.bfloat16),
                pltpu.VMEM((2, n, *block), jnp.bfloat16),
                pltpu.VMEM((2, n, *block), jnp.bfloat16),
                dma((2,)), dma((2, n, 2)), dma((2, n)), dma((2, n)), dma((2, n)),
            ]
        return pl.pallas_call(
            body,
            out_shape=(pltpu.VMEM((rows, width), jnp.float32),) * 2,
            in_specs=[pl.BlockSpec(memory_space=pltpu.HBM)] * 2
            + [pl.BlockSpec(memory_space=pltpu.SMEM)] * 2,
            out_specs=(pl.BlockSpec(memory_space=pltpu.VMEM),) * 2,
            scratch_shapes=scratch,
            compiler_params=pltpu.CompilerParams(
                collective_id=0, has_side_effects=True, vmem_limit_bytes=58 * 1024 * 1024
            ),
            cost_estimate=pl.CostEstimate(
                flops=16 * n * rows * rows * width,
                bytes_accessed=12 * rows * width,
                transcendentals=4 * n * rows * rows,
            ),
        )(image, text, scale, offset)

    return jax.shard_map(
        per_device,
        mesh=mesh,
        in_specs=(P(("outer", "inner"), None), P(("outer", "inner"), None), P(), P()),
        out_specs=(P(("outer", "inner"), None), P(("outer", "inner"), None)),
        check_vma=False,
    )
```
